32 devices in a mesh: slab: 8 (over y, x, core), pt: 4 (over z).
Axes of the slice: x: 2, y: 2, z: 4, core: 2. Of those that a mesh axis runs over, the one named last changes fastest.
Arguments:
- orbitals: bfloat16 [16384, 256], P('slab'), may hold values from -6 to 6
- potential: float32 [16384], P('slab'), may hold values from -1 to 1
- fit_matrix: bfloat16 [16384, 8192], P('slab', 'pt'), may hold values from -0.00390625 to 0.00390625
- owner_rows: int32 [4, 8, 512], P(None, 'slab'), may hold values from 0 to 2047, as said below
- owner_count: int32 [4, 8], replicated, may hold values from 0 to 512, as said below
Outputs:
- filtered: bfloat16 [16384, 256], P('slab')
The draws below stay inside these ranges and needn't reach their ends.
Inputs may be any that keep to these rules, and one draw needn't show every extreme that they name: `owner_count`: for each block p the counts over slabs sum to 2048, and in every block some slab lists exactly 512 points. `owner_rows`: the listed entries (c < owner_count[p, s]) of slab s are distinct over all blocks p and slots c; the other entries are 0.
All inputs are finite; a program needn't handle non-finite values.
Results may differ from the reference program's by a relative error of at most 0.0054.
Values may be sent and summed in bfloat16 or wider, within the bound.
A program may use at most 64 MiB of HBM per device.

```python
import jax
import jax.numpy as jnp
from jax import lax

NB = 256
NMU = 8192
DEG = 2
CZ = 8
NY = 8
NX = 32
G_DEV = 2048
NG = 16384
NMU_DEV = 2048
CAP = 512
N_SLAB = 8
N_PT = 4


def owner_layout(key):
    base_key = jax.random.fold_in(key, 7)
    key_big, key_weight, key_score, key_perm = jax.random.split(base_key, 4)
    slab_ids = jnp.arange(N_SLAB, dtype=jnp.int32)
    busiest = jax.random.randint(key_big, (N_PT,), 0, N_SLAB)
    is_big = slab_ids[None, :] == busiest[:, None]
    weights = jnp.where(is_big, 0, jax.random.randint(key_weight, (N_PT, N_SLAB), 2, 4))
    remaining = NMU_DEV - CAP
    shares = weights * remaining // jnp.sum(weights, axis=1, keepdims=True)
    leftover = remaining - jnp.sum(shares, axis=1, keepdims=True)
    scores = jax.random.randint(key_score, (N_PT, N_SLAB), 0, 1 << 20) * N_SLAB + slab_ids[None, :]
    scores = jnp.where(is_big, (1 << 20) * N_SLAB, scores)
    ranking = jnp.argsort(jnp.argsort(scores, axis=1), axis=1)
    counts = jnp.where(is_big, CAP, shares + (ranking < leftover).astype(jnp.int32)).astype(jnp.int32)

    def one_perm(perm_key):
        return jax.random.permutation(perm_key, G_DEV)
    permuted = jax.vmap(one_perm)(jax.random.split(key_perm, N_SLAB))
    starts = jnp.cumsum(counts, axis=0) - counts
    slot_ids = jnp.arange(CAP, dtype=jnp.int32)
    take_at = jnp.minimum(starts[:, :, None] + slot_ids[None, None, :], G_DEV - 1)
    picked = permuted[slab_ids[None, :, None], take_at]
    chosen = jnp.where(slot_ids[None, None, :] < counts[:, :, None], picked, 0)
    return (counts, chosen.astype(jnp.int32))


def draw_owner_rows(key, part):
    return owner_layout(key)[1]


def draw_owner_count(key, part):
    return owner_layout(key)[0]


def block_levels(rng, extent, cuts, smallest, largest):
    loudness = 1.0
    for position, blocks in cuts:
        draws = jax.random.uniform(jax.random.fold_in(jax.random.fold_in(rng, 6), position), (blocks,), jnp.float32, smallest / len(cuts), largest / len(cuts))
        loudness = loudness * jnp.repeat(jnp.exp(draws), extent[position] // blocks).reshape((-1,) + (1,) * (len(extent) - 1 - position))
    return loudness


def noise(own_key, extent, scale, limit, cuts=(), kind=jnp.bfloat16):
    values = jax.random.normal(own_key, extent, jnp.float32) * scale
    if len(cuts) > 0:
        values = block_levels(own_key, extent, cuts, -0.22, 0.18) * values
    return jnp.clip(values, min=-limit, max=limit).astype(kind)


def setup_inputs(seed: int = 0) -> dict:
    keys = jax.random.split(jax.random.key(seed), 6)
    orbitals = noise(keys[0], (NG, NB), 1.0, 6.0, ((0, 8),))
    potential = jnp.clip(jax.random.uniform(keys[1], (NG,), jnp.float32, -1.0, 1.0) * block_levels(keys[1], (NG,), ((0, 8),), -0.4, 0.0), -1.0, 1.0)
    fit_matrix = noise(keys[2], (NG, NMU), (NMU * NB) ** -0.5, 0.00390625, ((0, 8), (1, 4)))
    owner_rows = draw_owner_rows(jax.random.fold_in(keys[5], 71), 0)
    owner_count = draw_owner_count(jax.random.fold_in(keys[5], 71), 0)
    return dict(orbitals=orbitals, potential=potential, fit_matrix=fit_matrix, owner_rows=owner_rows, owner_count=owner_count)


stencil_coef = (-205.0 / 72.0, 8.0 / 5.0, -1.0 / 5.0, 8.0 / 315.0, -1.0 / 560.0)


def kinetic(vectors):
    blocked = vectors.astype(jnp.float32).reshape(CZ * N_SLAB, NY, NX, NB)
    summed = 3.0 * stencil_coef[0] * blocked
    for offset in range(1, 5):
        for axis_num in range(3):
            summed = summed + stencil_coef[offset] * (jnp.roll(blocked, offset, axis_num) + jnp.roll(blocked, -offset, axis_num))
    return (-0.5 * summed).reshape(CZ * N_SLAB * NY * NX, NB)


def point_index(owner_rows, owner_count):
    inclusive = jnp.cumsum(owner_count, axis=1).astype(jnp.int32)
    point_ranks = jnp.arange(NMU // N_PT, dtype=jnp.int32)
    before = (inclusive[:, None, :] <= point_ranks[None, :, None]).astype(jnp.int32)
    slab_of = jnp.sum(before, axis=2).astype(jnp.int32)
    base_count = jnp.sum(before * owner_count[:, None, :], axis=2).astype(jnp.int32)
    flat_rows = owner_rows.reshape(N_PT, N_SLAB * CAP)
    local_rows = jnp.take_along_axis(flat_rows, (slab_of * CAP + point_ranks[None, :] - base_count).astype(jnp.int32), axis=1)
    return (slab_of * (CZ * NY * NX) + local_rows).reshape(NMU).astype(jnp.int32)


def reference(orbitals, potential, fit_matrix, owner_rows, owner_count):
    slab_rows = CZ * NY * NX
    points = point_index(owner_rows, owner_count)
    psi_points = jnp.take(orbitals, points, axis=0).astype(jnp.float32)
    orbital_blocks = orbitals.reshape(N_SLAB, slab_rows, NB)
    fit_blocks = fit_matrix.reshape(N_SLAB, slab_rows, NMU)

    def kernel_block(tile_pair):
        fit_block, orbital_block = tile_pair
        density = jnp.dot(orbital_block.astype(jnp.float32), psi_points.T, preferred_element_type=jnp.float32)
        return (fit_block.astype(jnp.float32) * density).astype(jnp.bfloat16)

    kernel = lax.map(kernel_block, (fit_blocks, orbital_blocks))

    def apply_op(vectors):
        field_points = jnp.take(vectors, points, axis=0).astype(jnp.float32)

        def exch_block(kernel_tile):
            return jnp.dot(kernel_tile.astype(jnp.float32), field_points, preferred_element_type=jnp.float32)

        exch_term = lax.map(exch_block, kernel).reshape(N_SLAB * slab_rows, NB)
        return kinetic(vectors) + potential[:, None] * vectors.astype(jnp.float32) - exch_term

    previous = orbitals
    current = orbitals
    for turn_number in range(DEG):
        applied = apply_op(current)
        scaled = applied - 3.5 * current.astype(jnp.float32)
        if turn_number == 0:
            upcoming = (scaled / 4.0).astype(jnp.bfloat16)
        else:
            upcoming = (0.5 * scaled - previous.astype(jnp.float32)).astype(jnp.bfloat16)
        previous, current = current, upcoming
    return current
```

```python
import functools

import jax
import jax.numpy as jnp
import ml_dtypes
import numpy as np
from jax import lax
from jax.experimental import pallas as pl
from jax.experimental.pallas import tpu as pltpu
from jax.sharding import PartitionSpec as P

DEG = 2
NY = 8
NX = 32
PLANE = NY * NX
WIDTH = 4
ALIGN = 16
MESH = pl.DeviceIdType.MESH
VMEM_LIMIT = 48 * 1024 * 1024
CHUNK = 128
LAG = 2

stencil_coef = (-205.0 / 72.0, 8.0 / 5.0, -1.0 / 5.0, 8.0 / 315.0, -1.0 / 560.0)


def plane_table():
    cells = np.arange(PLANE)
    row_y, col_x = cells // NX, cells % NX
    diff_y = (row_y[:, None] - row_y[None, :]) % NY
    diff_x = (col_x[:, None] - col_x[None, :]) % NX
    same_y, same_x = diff_y == 0, diff_x == 0
    table = np.where(same_y & same_x, 3.0 * stencil_coef[0], 0.0)
    for offset in range(1, WIDTH + 1):
        for shift in (offset, -offset):
            table = table + stencil_coef[offset] * (same_y & (diff_x == shift % NX))
            table = table + stencil_coef[offset] * (same_x & (diff_y == shift % NY))
    terms, rest = [], table.astype(np.float32)
    for _ in range(3):
        term = rest.astype(ml_dtypes.bfloat16)
        terms.append(term)
        rest = rest - term.astype(np.float32)
    return np.concatenate(terms, axis=0)


def flipped(index, bit):
    size = 1 << bit
    return index + size - 2 * size * lax.rem(lax.div(index, size), 2)


def gather_kernel(bits, field, rows, out, send_sem, recv_sem):
    me = lax.axis_index("slab")
    barrier = pltpu.get_barrier_semaphore()
    for bit in range(bits):
        pl.semaphore_signal(
            barrier, inc=1, device_id={"slab": flipped(me, bit)}, device_id_type=MESH
        )
    count, cells = rows.shape[0], field.shape[0]
    half = field.shape[1] // 2
    cell_ids = lax.broadcasted_iota(jnp.int32, (count, cells), 1)
    chosen = jnp.where(rows[...] == cell_ids, 1.0, 0.0).astype(jnp.bfloat16)
    picked = jnp.dot(chosen, field[...], preferred_element_type=jnp.float32)
    out[0] = picked.astype(jnp.bfloat16)
    pl.semaphore_wait(barrier, bits)

    outer = list(range(1, bits))
    orders = (outer + [0], outer[::-1] + [0])

    def copy(h, slot, bit):
        columns = pl.ds(h * half, half)
        target = slot | (1 << bit)
        return pltpu.make_async_remote_copy(
            src_ref=out.at[slot, :, columns],
            dst_ref=out.at[target, :, columns],
            send_sem=send_sem.at[h, target],
            recv_sem=recv_sem.at[h, target],
            device_id={"slab": flipped(me, bit)},
            device_id_type=MESH,
        )

    copies = []
    queue = []
    for place in range(bits):
        for h in range(2):
            bit = orders[h][place]
            one = copy(h, 0, bit)
            one.start()
            copies.append(one)
            queue.append((h, 1 << bit, place, one))
    while queue:
        queue.sort(key=lambda item: (item[2] == bits - 1, bin(item[1]).count("1"), item[2]))
        h, slot, place, arrived = queue.pop(0)
        arrived.wait_recv()
        for later in range(place + 1, bits):
            bit = orders[h][later]
            one = copy(h, slot, bit)
            one.start()
            copies.append(one)
            queue.append((h, slot | (1 << bit), later, one))
    for one in copies:
        one.wait_send()


def gather_points(field, rows, slabs):
    bits = slabs.bit_length() - 1
    count, columns = rows.shape[0], field.shape[1]
    return pl.pallas_call(
        functools.partial(gather_kernel, bits),
        out_shape=jax.ShapeDtypeStruct((slabs, count, columns), jnp.bfloat16),
        in_specs=[pl.BlockSpec(memory_space=pltpu.VMEM)] * 2,
        out_specs=pl.BlockSpec(memory_space=pltpu.VMEM),
        scratch_shapes=[
            pltpu.SemaphoreType.DMA((2, slabs)),
            pltpu.SemaphoreType.DMA((2, slabs)),
        ],
        compiler_params=pltpu.CompilerParams(
            collective_id=0, has_side_effects=True, vmem_limit_bytes=VMEM_LIMIT
        ),
        cost_estimate=pl.CostEstimate(
            flops=2 * count * field.shape[0] * columns,
            bytes_accessed=2 * (slabs * count + field.shape[0]) * columns,
            transcendentals=0,
        ),
    )(field, rows)


def pack(starts, gathered, packed):
    slabs, count, _ = gathered.shape
    packed[...] = jnp.zeros_like(packed)

    def one(slot, carry):
        place = pl.ds(pl.multiple_of(starts[slot], ALIGN), count)
        packed[place, :] = packed[place, :] + gathered[slot]
        return carry

    lax.fori_loop(0, slabs, one, 0)


def density_kernel(starts, gathered, orbitals, fit, kernel, points, packed):
    total = points.shape[0]

    @pl.when(pl.program_id(0) == 0)
    def _():
        pack(starts, gathered, packed)
        points[...] = packed[:total, :]

    density = lax.dot_general(
        orbitals[...], points[...], (((1,), (1,)), ((), ())), preferred_element_type=jnp.float32
    )
    kernel[...] = (fit[...].astype(jnp.float32) * density).astype(jnp.bfloat16)


def density_and_points(starts, gathered, orbitals, fit):
    cells, total = fit.shape
    slabs, count, columns = gathered.shape
    block = 256
    whole = lambda i: (0, 0)
    return pl.pallas_call(
        density_kernel,
        grid=(cells // block,),
        out_shape=[
            jax.ShapeDtypeStruct((cells, total), jnp.bfloat16),
            jax.ShapeDtypeStruct((total, columns), jnp.bfloat16),
        ],
        in_specs=[
            pl.BlockSpec(memory_space=pltpu.SMEM),
            pl.BlockSpec((slabs, count, columns), lambda i: (0, 0, 0)),
            pl.BlockSpec((block, columns), lambda i: (i, 0)),
            pl.BlockSpec((block, total), lambda i: (i, 0)),
        ],
        out_specs=[
            pl.BlockSpec((block, total), lambda i: (i, 0)),
            pl.BlockSpec((total, columns), whole),
        ],
        scratch_shapes=[pltpu.VMEM((total + count, columns), jnp.bfloat16)],
        compiler_params=pltpu.CompilerParams(vmem_limit_bytes=VMEM_LIMIT),
        cost_estimate=pl.CostEstimate(
            flops=2 * cells * total * columns, bytes_accessed=4 * cells * total, transcendentals=0
        ),
    )(starts, gathered, orbitals, fit)


def pack_kernel(starts, gathered, points, packed):
    pack(starts, gathered, packed)
    points[...] = packed[: points.shape[0], :]


def packed_points(starts, gathered, total):
    slabs, count, columns = gathered.shape
    return pl.pallas_call(
        pack_kernel,
        out_shape=jax.ShapeDtypeStruct((total, columns), jnp.bfloat16),
        in_specs=[
            pl.BlockSpec(memory_space=pltpu.SMEM),
            pl.BlockSpec(memory_space=pltpu.VMEM),
        ],
        out_specs=pl.BlockSpec(memory_space=pltpu.VMEM),
        scratch_shapes=[pltpu.VMEM((total + count, columns), jnp.bfloat16)],
        compiler_params=pltpu.CompilerParams(vmem_limit_bytes=VMEM_LIMIT),
    )(starts, gathered)


def apply_kernel(
    first, n, slabs, kernel, points, field, prev, pot, table, out,
    kbuf, part, ext, base, sent, got, ksem, red_send, red_recv, bc_send, bc_recv, halo_send, halo_recv,
):
    z = lax.axis_index("pt")
    s = lax.axis_index("slab")
    cells, columns = out.shape
    half = columns // 2
    chunks = cells // CHUNK
    block = 2 * CHUNK
    rim = WIDTH * PLANE
    scale = 0.25 if first else 0.5
    is_end = (z == 0) | (z == n - 1)
    upper = lax.rem(s + 1, slabs)
    lower = lax.rem(s + slabs - 1, slabs)

    def fetch(i):
        rows = pl.ds(pl.multiple_of(i * block, block), block)
        return pltpu.make_async_copy(kernel.at[rows, :], kbuf.at[rows, :], ksem.at[i])

    def fetch_start(i, carry):
        fetch(i).start()
        return carry

    lax.fori_loop(0, cells // block, fetch_start, 0)

    barrier = pltpu.get_barrier_semaphore()

    @pl.when(z > 0)
    def _():
        pl.semaphore_signal(barrier, inc=1, device_id={"pt": z - 1}, device_id_type=MESH)

    @pl.when(z < n - 1)
    def _():
        pl.semaphore_signal(barrier, inc=1, device_id={"pt": z + 1}, device_id_type=MESH)

    @pl.when(is_end)
    def _():
        pl.semaphore_signal(barrier, inc=1, device_id={"slab": upper}, device_id_type=MESH)
        pl.semaphore_signal(barrier, inc=1, device_id={"slab": lower}, device_id_type=MESH)
        pl.semaphore_wait(barrier, 3)

    @pl.when(jnp.logical_not(is_end))
    def _():
        pl.semaphore_wait(barrier, 2)

    def halo(k):
        src, dst, to = ((cells, 0, upper), (rim, rim + cells, lower))[k]
        return pltpu.make_async_remote_copy(
            src_ref=ext.at[pl.ds(src, rim), :],
            dst_ref=ext.at[pl.ds(dst, rim), :],
            send_sem=halo_send.at[k],
            recv_sem=halo_recv.at[k],
            device_id={"slab": to},
            device_id_type=MESH,
        )

    own = pl.ds(pl.multiple_of(jnp.where(z == 0, 0, half), half), half)

    @pl.when(is_end)
    def _():
        ext[rim : rim + cells, :] = field[:, own]
        halo(0).start()
        halo(1).start()

    def reduce_copy(h, c, to):
        rows = pl.ds(pl.multiple_of(c * CHUNK, CHUNK), CHUNK)
        return pltpu.make_async_remote_copy(
            src_ref=sent.at[h, rows, :],
            dst_ref=got.at[h, rows, :],
            send_sem=red_send.at[h, c],
            recv_sem=red_recv.at[h, c],
            device_id={"pt": to},
            device_id_type=MESH,
        )

    def result_copy(h, c, to):
        rows = pl.ds(pl.multiple_of(c * CHUNK, CHUNK), CHUNK)
        view = out.at[rows, pl.ds(h * half, half)]
        return pltpu.make_async_remote_copy(
            src_ref=view,
            dst_ref=view,
            send_sem=bc_send.at[h, c],
            recv_sem=bc_recv.at[h, c],
            device_id={"pt": to},
            device_id_type=MESH,
        )

    sides = []
    for h in range(2):
        far = n - 1 - z if h == 0 else z
        near = z if h == 0 else n - 1 - z
        toward = z - 1 if h == 0 else z + 1
        away = z + 1 if h == 0 else z - 1
        sides.append((far, near, toward, away))

    def local_terms():
        for k in range(2):
            halo(k).wait()

        def one(k, carry):
            def plane(i):
                return ext[pl.ds(pl.multiple_of((k + WIDTH + i) * PLANE, PLANE), PLANE), :]

            rows = pl.ds(pl.multiple_of(k * PLANE, PLANE), PLANE)
            centre = plane(0)
            terms = jnp.dot(table[...], centre, preferred_element_type=jnp.float32)
            summed = terms[:PLANE] + (terms[PLANE : 2 * PLANE] + terms[2 * PLANE :])
            for offset in range(1, WIDTH + 1):
                pair = plane(offset).astype(jnp.float32) + plane(-offset).astype(jnp.float32)
                summed = summed + stencil_coef[offset] * pair
            value = scale * (-0.5 * summed + (pot[rows, :] - 3.5) * centre.astype(jnp.float32))
            if not first:
                value = value - prev[rows, own].astype(jnp.float32)
            base[rows, :] = value
            return carry

        lax.fori_loop(0, cells // PLANE, one, 0)

    def step(t, carry):
        @pl.when((lax.rem(t, 2) == 0) & (t < chunks))
        def _():
            i = lax.div(t, 2)
            fetch(i).wait()
            rows = pl.ds(pl.multiple_of(i * block, block), block)
            part[rows, :] = jnp.dot(
                kbuf[rows, :], points[...], preferred_element_type=jnp.float32
            )

        @pl.when((t == LAG * (n - 1)) & is_end)
        def _():
            local_terms()

        for h, (far, near, toward, away) in enumerate(sides):
            cols = pl.ds(h * half, half)
            c = t - LAG * far

            @pl.when((c >= 0) & (c < chunks))
            def _():
                rows = pl.ds(pl.multiple_of(c * CHUNK, CHUNK), CHUNK)

                @pl.when(far > 0)
                def _():
                    reduce_copy(h, c, away).wait_recv()
                    part[rows, cols] = part[rows, cols] + got[h, rows, :].astype(jnp.float32)

                @pl.when(near > 0)
                def _():
                    sent[h, rows, :] = part[rows, cols].astype(jnp.bfloat16)
                    reduce_copy(h, c, toward).start()

                @pl.when(near == 0)
                def _():
                    out[rows, cols] = (base[rows, :] - scale * part[rows, cols]).astype(jnp.bfloat16)
                    result_copy(h, c, away).start()

            b = t - LAG * (n - 1) - LAG * near

            @pl.when((near > 0) & (b >= 0) & (b < chunks))
            def _():
                result_copy(h, b, toward).wait_recv()

                @pl.when(far > 0)
                def _():
                    result_copy(h, b, away).start()

        return carry

    lax.fori_loop(0, chunks + 2 * LAG * (n - 1), step, 0)

    def finish(c, carry):
        for h, (far, near, toward, away) in enumerate(sides):
            @pl.when(near > 0)
            def _():
                reduce_copy(h, c, toward).wait_send()

            @pl.when(far > 0)
            def _():
                result_copy(h, c, away).wait_send()

        return carry

    lax.fori_loop(0, chunks, finish, 0)


def apply_turn(first, n, slabs, kernel, points, field, prev, pot, table):
    cells, total = kernel.shape
    columns = field.shape[1]
    half = columns // 2
    chunks = cells // CHUNK
    vmem = pl.BlockSpec(memory_space=pltpu.VMEM)
    return pl.pallas_call(
        functools.partial(apply_kernel, first, n, slabs),
        out_shape=jax.ShapeDtypeStruct((cells, columns), jnp.bfloat16),
        in_specs=[pl.BlockSpec(memory_space=pl.ANY)] + [vmem] * 5,
        out_specs=vmem,
        scratch_shapes=[
            pltpu.VMEM((cells, total), jnp.bfloat16),
            pltpu.VMEM((cells, columns), jnp.float32),
            pltpu.VMEM((cells + 2 * WIDTH * PLANE, half), jnp.bfloat16),
            pltpu.VMEM((cells, half), jnp.float32),
            pltpu.VMEM((2, cells, half), jnp.bfloat16),
            pltpu.VMEM((2, cells, half), jnp.bfloat16),
            pltpu.SemaphoreType.DMA((chunks // 2,)),
            pltpu.SemaphoreType.DMA((2, chunks)),
            pltpu.SemaphoreType.DMA((2, chunks)),
            pltpu.SemaphoreType.DMA((2, chunks)),
            pltpu.SemaphoreType.DMA((2, chunks)),
            pltpu.SemaphoreType.DMA((2,)),
            pltpu.SemaphoreType.DMA((2,)),
        ],
        compiler_params=pltpu.CompilerParams(
            collective_id=1 if first else 2, has_side_effects=True, vmem_limit_bytes=VMEM_LIMIT
        ),
        cost_estimate=pl.CostEstimate(
            flops=2 * cells * total * columns, bytes_accessed=2 * cells * total, transcendentals=0
        ),
    )(kernel, points, field, prev, pot, table)


def shifted_rows(owner_rows, owner_count, block_index, slabs):
    me = lax.axis_index("slab")
    capacity = owner_rows.shape[2]
    mine = lax.dynamic_index_in_dim(owner_rows[:, 0, :], block_index, 0, keepdims=False)
    counts = lax.dynamic_index_in_dim(owner_count, block_index, 0, keepdims=False)
    places = jnp.cumsum(counts) - counts
    listed = jnp.where(jnp.arange(capacity, dtype=jnp.int32) < counts[me], mine, -1)
    filler = jnp.full((ALIGN,), -1, jnp.int32)
    padded = jnp.concatenate([filler, listed, filler])
    rows = lax.dynamic_slice_in_dim(padded, ALIGN - places[me] % ALIGN, capacity + ALIGN, 0)
    slots = jnp.bitwise_xor(jnp.arange(slabs, dtype=jnp.int32), me)
    starts = jnp.take(places // ALIGN * ALIGN, slots, axis=0)
    return rows[:, None], starts.astype(jnp.int32)


def body(n, slabs, orbitals, potential, fit_matrix, owner_rows, owner_count):
    block_index = lax.axis_index("pt")
    rows, starts = shifted_rows(owner_rows, owner_count, block_index, slabs)
    pot = potential[:, None]
    table = jnp.asarray(plane_table())
    gathered = gather_points(orbitals, rows, slabs)
    kernel, points = density_and_points(starts, gathered, orbitals, fit_matrix)
    previous = current = orbitals
    for turn in range(DEG):
        upcoming = apply_turn(turn == 0, n, slabs, kernel, points, current, previous, pot, table)
        previous, current = current, upcoming
        if turn + 1 < DEG:
            gathered = gather_points(current, rows, slabs)
            points = packed_points(starts, gathered, points.shape[0])
    return current


def solution(mesh):
    placed = (P("slab", None), P("slab"), P("slab", "pt"), P(None, "slab", None), P())
    return jax.shard_map(
        functools.partial(body, mesh.shape["pt"], mesh.shape["slab"]),
        mesh=mesh, in_specs=placed, out_specs=P("slab", None), check_vma=False,
    )
```

```python
import functools

import jax
import jax.numpy as jnp
import ml_dtypes
import numpy as np
from jax import lax
from jax.experimental import pallas as pl
from jax.experimental.pallas import tpu as pltpu
from jax.sharding import PartitionSpec as P

DEG = 2
NY = 8
NX = 32
PLANE = NY * NX
WIDTH = 4
ALIGN = 16
MESH = pl.DeviceIdType.MESH
VMEM_LIMIT = 48 * 1024 * 1024
BLOCK = 256
CHUNK = 64
LAG = 3

stencil_coef = (-205.0 / 72.0, 8.0 / 5.0, -1.0 / 5.0, 8.0 / 315.0, -1.0 / 560.0)


def plane_table():
    cells = np.arange(PLANE)
    row_y, col_x = cells // NX, cells % NX
    diff_y = (row_y[:, None] - row_y[None, :]) % NY
    diff_x = (col_x[:, None] - col_x[None, :]) % NX
    same_y, same_x = diff_y == 0, diff_x == 0
    table = np.where(same_y & same_x, 3.0 * stencil_coef[0], 0.0)
    for offset in range(1, WIDTH + 1):
        for shift in (offset, -offset):
            table = table + stencil_coef[offset] * (same_y & (diff_x == shift % NX))
            table = table + stencil_coef[offset] * (same_x & (diff_y == shift % NY))
    terms, rest = [], table.astype(np.float32)
    for _ in range(3):
        term = rest.astype(ml_dtypes.bfloat16)
        terms.append(term)
        rest = rest - term.astype(np.float32)
    return np.concatenate(terms, axis=0)


def flipped(index, bit):
    size = 1 << bit
    return index + size - 2 * size * lax.rem(lax.div(index, size), 2)


def gather_kernel(bits, field, rows, out, send_sem, recv_sem):
    me = lax.axis_index("slab")
    barrier = pltpu.get_barrier_semaphore()
    for bit in range(bits):
        pl.semaphore_signal(
            barrier, inc=1, device_id={"slab": flipped(me, bit)}, device_id_type=MESH
        )
    count, cells = rows.shape[0], field.shape[0]
    half = field.shape[1] // 2
    cell_ids = lax.broadcasted_iota(jnp.int32, (count, cells), 1)
    chosen = jnp.where(rows[...] == cell_ids, 1.0, 0.0).astype(jnp.bfloat16)
    picked = jnp.dot(chosen, field[...], preferred_element_type=jnp.float32)
    out[0] = picked.astype(jnp.bfloat16)
    pl.semaphore_wait(barrier, bits)

    outer = list(range(1, bits))
    orders = (outer + [0], outer[::-1] + [0])

    def copy(h, slot, bit):
        columns = pl.ds(h * half, half)
        target = slot | (1 << bit)
        return pltpu.make_async_remote_copy(
            src_ref=out.at[slot, :, columns],
            dst_ref=out.at[target, :, columns],
            send_sem=send_sem.at[h, target],
            recv_sem=recv_sem.at[h, target],
            device_id={"slab": flipped(me, bit)},
            device_id_type=MESH,
        )

    copies = []
    queue = []
    for place in range(bits):
        for h in range(2):
            bit = orders[h][place]
            one = copy(h, 0, bit)
            one.start()
            copies.append(one)
            queue.append((h, 1 << bit, place, one))
    while queue:
        queue.sort(key=lambda item: (item[2] == bits - 1, bin(item[1]).count("1"), item[2]))
        h, slot, place, arrived = queue.pop(0)
        arrived.wait_recv()
        for later in range(place + 1, bits):
            bit = orders[h][later]
            one = copy(h, slot, bit)
            one.start()
            copies.append(one)
            queue.append((h, slot | (1 << bit), later, one))
    for one in copies:
        one.wait_send()


def gather_points(field, rows, slabs):
    bits = slabs.bit_length() - 1
    count, columns = rows.shape[0], field.shape[1]
    return pl.pallas_call(
        functools.partial(gather_kernel, bits),
        out_shape=jax.ShapeDtypeStruct((slabs, count, columns), jnp.bfloat16),
        in_specs=[pl.BlockSpec(memory_space=pltpu.VMEM)] * 2,
        out_specs=pl.BlockSpec(memory_space=pltpu.VMEM),
        scratch_shapes=[
            pltpu.SemaphoreType.DMA((2, slabs)),
            pltpu.SemaphoreType.DMA((2, slabs)),
        ],
        compiler_params=pltpu.CompilerParams(
            collective_id=0, has_side_effects=True, vmem_limit_bytes=VMEM_LIMIT
        ),
        cost_estimate=pl.CostEstimate(
            flops=2 * count * field.shape[0] * columns,
            bytes_accessed=2 * (slabs * count + field.shape[0]) * columns,
            transcendentals=0,
        ),
    )(field, rows)


def pack(starts, gathered, packed):
    slabs, count, _ = gathered.shape
    packed[...] = jnp.zeros_like(packed)

    def one(slot, carry):
        place = pl.ds(pl.multiple_of(starts[slot], ALIGN), count)
        packed[place, :] = packed[place, :] + gathered[slot]
        return carry

    lax.fori_loop(0, slabs, one, 0)


def pack_kernel(with_transpose, starts, gathered, points, *rest):
    packed = rest[-1]
    pack(starts, gathered, packed)
    value = packed[: points.shape[0], :]
    points[...] = value
    if with_transpose:
        rest[0][...] = value.T


def packed_points(starts, gathered, total, with_transpose):
    slabs, count, columns = gathered.shape
    vmem = pl.BlockSpec(memory_space=pltpu.VMEM)
    shapes = [jax.ShapeDtypeStruct((total, columns), jnp.bfloat16)]
    if with_transpose:
        shapes.append(jax.ShapeDtypeStruct((columns, total), jnp.bfloat16))
    return pl.pallas_call(
        functools.partial(pack_kernel, with_transpose),
        out_shape=shapes,
        in_specs=[pl.BlockSpec(memory_space=pltpu.SMEM), vmem],
        out_specs=[vmem] * len(shapes),
        scratch_shapes=[pltpu.VMEM((total + count, columns), jnp.bfloat16)],
        compiler_params=pltpu.CompilerParams(vmem_limit_bytes=VMEM_LIMIT),
    )(starts, gathered)


def apply_kernel(first, n, slabs, *refs):
    if first:
        source, points, points_t, field, pot, table, out, kernel_out = refs[:8]
        rest = refs[8:]
        prev = None
    else:
        source, points, field, prev, pot, table, out = refs[:7]
        rest = refs[7:]
    (kbuf, part, ext, base, sent, got, ksem, osem,
     red_send, red_recv, bc_send, bc_recv, halo_send, halo_recv) = rest
    z = lax.axis_index("pt")
    s = lax.axis_index("slab")
    cells, columns = out.shape
    half = columns // 2
    chunks = cells // CHUNK
    per_block = BLOCK // CHUNK
    per_plane = PLANE // CHUNK
    rim = WIDTH * PLANE
    scale = 0.25 if first else 0.5
    owners = (n // 2 - 1, n // 2)
    depth = n // 2
    is_owner = (z == owners[0]) | (z == owners[1])
    upper = lax.rem(s + 1, slabs)
    lower = lax.rem(s + slabs - 1, slabs)

    def block_rows(i):
        return pl.ds(pl.multiple_of(i * BLOCK, BLOCK), BLOCK)

    def fetch(i):
        rows = block_rows(i)
        return pltpu.make_async_copy(source.at[rows, :], kbuf.at[rows, :], ksem.at[i])

    def keep(i):
        rows = block_rows(i)
        return pltpu.make_async_copy(kbuf.at[rows, :], kernel_out.at[rows, :], osem.at[i])

    def fetch_start(i, carry):
        fetch(i).start()
        return carry

    lax.fori_loop(0, cells // BLOCK, fetch_start, 0)

    barrier = pltpu.get_barrier_semaphore()

    @pl.when(z > 0)
    def _():
        pl.semaphore_signal(barrier, inc=1, device_id={"pt": z - 1}, device_id_type=MESH)

    @pl.when(z < n - 1)
    def _():
        pl.semaphore_signal(barrier, inc=1, device_id={"pt": z + 1}, device_id_type=MESH)

    @pl.when(is_owner)
    def _():
        pl.semaphore_signal(barrier, inc=1, device_id={"slab": upper}, device_id_type=MESH)
        pl.semaphore_signal(barrier, inc=1, device_id={"slab": lower}, device_id_type=MESH)

    greeted = jnp.where(is_owner, 2, 0) + jnp.where(z > 0, 1, 0) + jnp.where(z < n - 1, 1, 0)
    pl.semaphore_wait(barrier, greeted)

    def halo(k):
        src, dst, to = ((cells, 0, upper), (rim, rim + cells, lower))[k]
        return pltpu.make_async_remote_copy(
            src_ref=ext.at[pl.ds(src, rim), :],
            dst_ref=ext.at[pl.ds(dst, rim), :],
            send_sem=halo_send.at[k],
            recv_sem=halo_recv.at[k],
            device_id={"slab": to},
            device_id_type=MESH,
        )

    own = pl.ds(pl.multiple_of(jnp.where(z == owners[0], 0, half), half), half)

    @pl.when(is_owner)
    def _():
        ext[rim : rim + cells, :] = field[:, own]
        halo(0).start()
        halo(1).start()

    def chunk_rows(c):
        return pl.ds(pl.multiple_of(c * CHUNK, CHUNK), CHUNK)

    def reduce_copy(h, side, c, to):
        rows = chunk_rows(c)
        return pltpu.make_async_remote_copy(
            src_ref=sent.at[h, rows, :],
            dst_ref=got.at[h, side, rows, :],
            send_sem=red_send.at[h, c],
            recv_sem=red_recv.at[h, side, c],
            device_id={"pt": to},
            device_id_type=MESH,
        )

    def result_copy(h, side, c, to):
        view = out.at[chunk_rows(c), pl.ds(h * half, half)]
        return pltpu.make_async_remote_copy(
            src_ref=view,
            dst_ref=view,
            send_sem=bc_send.at[h, side, c],
            recv_sem=bc_recv.at[h, c],
            device_id={"pt": to},
            device_id_type=MESH,
        )

    def local_plane(k):
        def plane(i):
            return ext[pl.ds(pl.multiple_of((k + WIDTH + i) * PLANE, PLANE), PLANE), :]

        rows = pl.ds(pl.multiple_of(k * PLANE, PLANE), PLANE)
        centre = plane(0)
        terms = jnp.dot(table[...], centre, preferred_element_type=jnp.float32)
        summed = terms[:PLANE] + (terms[PLANE : 2 * PLANE] + terms[2 * PLANE :])
        for offset in range(1, WIDTH + 1):
            pair = plane(offset).astype(jnp.float32) + plane(-offset).astype(jnp.float32)
            summed = summed + stencil_coef[offset] * pair
        level = jnp.broadcast_to(pot[pl.ds(k, 1), :], (8, PLANE)).T[:, :1]
        value = scale * (-0.5 * summed + (level - 3.5) * centre.astype(jnp.float32))
        if prev is not None:
            value = value - prev[rows, own].astype(jnp.float32)
        base[rows, :] = value

    def step(t, carry):
        @pl.when((lax.rem(t, per_block) == 0) & (t < chunks))
        def _():
            i = lax.div(t, per_block)
            fetch(i).wait()
            rows = block_rows(i)
            if first:
                density = jnp.dot(
                    field[rows, :], points_t[...], preferred_element_type=jnp.float32
                )
                kbuf[rows, :] = (kbuf[rows, :].astype(jnp.float32) * density).astype(jnp.bfloat16)
                keep(i).start()
            part[rows, :] = jnp.dot(
                kbuf[rows, :], points[...], preferred_element_type=jnp.float32
            )

        o = t - LAG * depth

        @pl.when(is_owner & (o == 0))
        def _():
            halo(0).wait()
            halo(1).wait()

        @pl.when(is_owner & (o >= 0) & (o < chunks) & (lax.rem(o + chunks, per_plane) == 0))
        def _():
            local_plane(lax.div(o, per_plane))

        for h, owner in enumerate(owners):
            cols = pl.ds(h * half, half)

            for side in range(2):
                level = z if side == 0 else n - 1 - z
                inside = (z < owner) if side == 0 else (z > owner)
                back = z - 1 if side == 0 else z + 1
                ahead = z + 1 if side == 0 else z - 1
                c = t - LAG * level

                @pl.when(inside & (c >= 0) & (c < chunks))
                def _():
                    rows = chunk_rows(c)
                    value = part[rows, cols]

                    @pl.when(level == 0)
                    def _():
                        sent[h, rows, :] = value.astype(jnp.bfloat16)

                    @pl.when(level > 0)
                    def _():
                        reduce_copy(h, side, c, back).wait_recv()
                        total = value + got[h, side, rows, :].astype(jnp.float32)
                        sent[h, rows, :] = total.astype(jnp.bfloat16)

                    reduce_copy(h, side, c, ahead).start()

            @pl.when((z == owner) & (o >= 0) & (o < chunks))
            def _():
                rows = chunk_rows(o)
                total = part[rows, cols]
                if owner > 0:
                    reduce_copy(h, 0, o, z - 1).wait_recv()
                    total = total + got[h, 0, rows, :].astype(jnp.float32)
                if owner < n - 1:
                    reduce_copy(h, 1, o, z + 1).wait_recv()
                    total = total + got[h, 1, rows, :].astype(jnp.float32)
                out[rows, cols] = (base[rows, :] - scale * total).astype(jnp.bfloat16)
                if owner > 0:
                    result_copy(h, 0, o, z - 1).start()
                if owner < n - 1:
                    result_copy(h, 1, o, z + 1).start()

            for side in range(2):
                inside = (z < owner) if side == 0 else (z > owner)
                away = owner - z if side == 0 else z - owner
                back = z + 1 if side == 0 else z - 1
                ahead = z - 1 if side == 0 else z + 1
                more = (z > 0) if side == 0 else (z < n - 1)
                b = o - LAG * away

                @pl.when(inside & (b >= 0) & (b < chunks))
                def _():
                    result_copy(h, side, b, back).wait_recv()

                    @pl.when(more)
                    def _():
                        result_copy(h, side, b, ahead).start()

        return carry

    lax.fori_loop(0, chunks + 2 * LAG * depth, step, 0)

    def finish(c, carry):
        for h, owner in enumerate(owners):
            @pl.when(z < owner)
            def _():
                reduce_copy(h, 0, c, z + 1).wait_send()

            @pl.when(z > owner)
            def _():
                reduce_copy(h, 1, c, z - 1).wait_send()

            @pl.when((z <= owner) & (z > 0))
            def _():
                result_copy(h, 0, c, z - 1).wait_send()

            @pl.when((z >= owner) & (z < n - 1))
            def _():
                result_copy(h, 1, c, z + 1).wait_send()

        return carry

    lax.fori_loop(0, chunks, finish, 0)
    if first:
        def kept(i, carry):
            keep(i).wait()
            return carry

        lax.fori_loop(0, cells // BLOCK, kept, 0)


def apply_turn(first, n, slabs, source, operands):
    cells, total = source.shape
    columns = operands[0].shape[1]
    half = columns // 2
    chunks = cells // CHUNK
    blocks = cells // BLOCK
    vmem = pl.BlockSpec(memory_space=pltpu.VMEM)
    anywhere = pl.BlockSpec(memory_space=pl.ANY)
    shapes = [jax.ShapeDtypeStruct((cells, columns), jnp.bfloat16)]
    if first:
        shapes.append(jax.ShapeDtypeStruct((cells, total), jnp.bfloat16))
    return pl.pallas_call(
        functools.partial(apply_kernel, first, n, slabs),
        out_shape=shapes,
        in_specs=[anywhere] + [vmem] * len(operands),
        out_specs=[vmem, anywhere][: len(shapes)],
        scratch_shapes=[
            pltpu.VMEM((cells, total), jnp.bfloat16),
            pltpu.VMEM((cells, columns), jnp.float32),
            pltpu.VMEM((cells + 2 * WIDTH * PLANE, half), jnp.bfloat16),
            pltpu.VMEM((cells, half), jnp.float32),
            pltpu.VMEM((2, cells, half), jnp.bfloat16),
            pltpu.VMEM((2, 2, cells, half), jnp.bfloat16),
            pltpu.SemaphoreType.DMA((blocks,)),
            pltpu.SemaphoreType.DMA((blocks,)),
            pltpu.SemaphoreType.DMA((2, chunks)),
            pltpu.SemaphoreType.DMA((2, 2, chunks)),
            pltpu.SemaphoreType.DMA((2, 2, chunks)),
            pltpu.SemaphoreType.DMA((2, chunks)),
            pltpu.SemaphoreType.DMA((2,)),
            pltpu.SemaphoreType.DMA((2,)),
        ],
        compiler_params=pltpu.CompilerParams(
            collective_id=1 if first else 2, has_side_effects=True, vmem_limit_bytes=VMEM_LIMIT
        ),
        cost_estimate=pl.CostEstimate(
            flops=2 * cells * total * columns, bytes_accessed=2 * cells * total, transcendentals=0
        ),
    )(source, *operands)


def rows_kernel(counts, listed, rows, starts, wide):
    z = lax.axis_index("pt")
    me = lax.axis_index("slab")
    slabs = counts.shape[1]
    capacity = listed.shape[2]

    def one(s, carry):
        place, mine = carry
        starts[lax.bitwise_xor(s, me)] = lax.div(place, ALIGN) * ALIGN
        mine = jnp.where(s == me, place, mine)
        return place + counts[z, s], mine

    _, mine = lax.fori_loop(0, slabs, one, (jnp.int32(0), jnp.int32(0)))
    lane = lax.broadcasted_iota(jnp.int32, (8, capacity), 1)
    value = jnp.broadcast_to(listed[z], (8, capacity))
    wide[...] = jnp.full(wide.shape, -1.0, jnp.float32)
    wide[:, :capacity] = jnp.where(lane < counts[z, me], value, -1).astype(jnp.float32)
    moved = pltpu.roll(wide[...], lax.rem(mine, ALIGN), 1)
    rows[...] = moved.T[: rows.shape[0], :1].astype(jnp.int32)


def shifted_rows(owner_rows, owner_count):
    slabs = owner_count.shape[1]
    count = owner_rows.shape[2] + ALIGN
    width = (count + 127) // 128 * 128
    smem = pl.BlockSpec(memory_space=pltpu.SMEM)
    vmem = pl.BlockSpec(memory_space=pltpu.VMEM)
    return pl.pallas_call(
        rows_kernel,
        out_shape=[
            jax.ShapeDtypeStruct((count, 1), jnp.int32),
            jax.ShapeDtypeStruct((slabs,), jnp.int32),
        ],
        in_specs=[smem, vmem],
        out_specs=[vmem, smem],
        scratch_shapes=[pltpu.VMEM((8, width), jnp.float32)],
    )(owner_count, owner_rows)


def body(n, slabs, orbitals, potential, fit_matrix, owner_rows, owner_count):
    rows, starts = shifted_rows(owner_rows, owner_count)
    pot = potential.reshape(-1, PLANE)
    table = jnp.asarray(plane_table())
    total = fit_matrix.shape[1]
    gathered = gather_points(orbitals, rows, slabs)
    points, points_t = packed_points(starts, gathered, total, True)
    current, kernel = apply_turn(
        True, n, slabs, fit_matrix, (points, points_t, orbitals, pot, table)
    )
    previous = orbitals
    for _ in range(1, DEG):
        gathered = gather_points(current, rows, slabs)
        (points,) = packed_points(starts, gathered, total, False)
        (upcoming,) = apply_turn(
            False, n, slabs, kernel, (points, current, previous, pot, table)
        )
        previous, current = current, upcoming
    return current


def solution(mesh):
    placed = (P("slab", None), P("slab"), P("slab", "pt"), P(None, "slab", None), P())
    return jax.shard_map(
        functools.partial(body, mesh.shape["pt"], mesh.shape["slab"]),
        mesh=mesh, in_specs=placed, out_specs=P("slab", None), check_vma=False,
    )
```

```python
import functools

import jax
import jax.numpy as jnp
import ml_dtypes
import numpy as np
from jax import lax
from jax.experimental import pallas as pl
from jax.experimental.pallas import tpu as pltpu
from jax.sharding import PartitionSpec as P

DEG = 2
NY = 8
NX = 32
PLANE = NY * NX
WIDTH = 4
ALIGN = 16
MESH = pl.DeviceIdType.MESH
VMEM_LIMIT = 48 * 1024 * 1024
BLOCK = 256
CHUNK = 64
LAG = 6

stencil_coef = (-205.0 / 72.0, 8.0 / 5.0, -1.0 / 5.0, 8.0 / 315.0, -1.0 / 560.0)


def plane_table():
    cells = np.arange(PLANE)
    row_y, col_x = cells // NX, cells % NX
    diff_y = (row_y[:, None] - row_y[None, :]) % NY
    diff_x = (col_x[:, None] - col_x[None, :]) % NX
    same_y, same_x = diff_y == 0, diff_x == 0
    table = np.where(same_y & same_x, 3.0 * stencil_coef[0], 0.0)
    for offset in range(1, WIDTH + 1):
        for shift in (offset, -offset):
            table = table + stencil_coef[offset] * (same_y & (diff_x == shift % NX))
            table = table + stencil_coef[offset] * (same_x & (diff_y == shift % NY))
    terms, rest = [], table.astype(np.float32)
    for _ in range(3):
        term = rest.astype(ml_dtypes.bfloat16)
        terms.append(term)
        rest = rest - term.astype(np.float32)
    return np.concatenate(terms, axis=0)


def flipped(index, bit):
    size = 1 << bit
    return index + size - 2 * size * lax.rem(lax.div(index, size), 2)


def gather_kernel(bits, staged, source, rows, out, send_sem, recv_sem, *stage):
    me = lax.axis_index("slab")
    field = source
    if staged:
        field = stage[0]
        inward = pltpu.make_async_copy(source, field, stage[1])
        inward.start()
    barrier = pltpu.get_barrier_semaphore()
    for bit in range(bits):
        pl.semaphore_signal(
            barrier, inc=1, device_id={"slab": flipped(me, bit)}, device_id_type=MESH
        )
    count, cells = rows.shape[0], field.shape[0]
    half = field.shape[1] // 2
    cell_ids = lax.broadcasted_iota(jnp.int32, (count, cells), 1)
    chosen = jnp.where(rows[...] == cell_ids, 1.0, 0.0).astype(jnp.bfloat16)
    if staged:
        inward.wait()
    picked = jnp.dot(chosen, field[...], preferred_element_type=jnp.float32)
    out[0] = picked.astype(jnp.bfloat16)
    pl.semaphore_wait(barrier, bits)

    outer = list(range(1, bits))
    orders = (outer + [0], outer[::-1] + [0])

    def copy(h, slot, bit):
        columns = pl.ds(h * half, half)
        target = slot | (1 << bit)
        return pltpu.make_async_remote_copy(
            src_ref=out.at[slot, :, columns],
            dst_ref=out.at[target, :, columns],
            send_sem=send_sem.at[h, target],
            recv_sem=recv_sem.at[h, target],
            device_id={"slab": flipped(me, bit)},
            device_id_type=MESH,
        )

    copies = []
    queue = []
    for place in range(bits):
        for h in range(2):
            bit = orders[h][place]
            one = copy(h, 0, bit)
            one.start()
            copies.append(one)
            queue.append((h, 1 << bit, place, one))
    while queue:
        queue.sort(key=lambda item: (item[2] == bits - 1, bin(item[1]).count("1"), item[2]))
        h, slot, place, arrived = queue.pop(0)
        arrived.wait_recv()
        for later in range(place + 1, bits):
            bit = orders[h][later]
            one = copy(h, slot, bit)
            one.start()
            copies.append(one)
            queue.append((h, slot | (1 << bit), later, one))
    for one in copies:
        one.wait_send()


def gather_points(field, rows, slabs, staged):
    bits = slabs.bit_length() - 1
    count, columns = rows.shape[0], field.shape[1]
    vmem = pl.BlockSpec(memory_space=pltpu.VMEM)
    stage = [pltpu.VMEM(field.shape, field.dtype), pltpu.SemaphoreType.DMA] if staged else []
    return pl.pallas_call(
        functools.partial(gather_kernel, bits, staged),
        out_shape=jax.ShapeDtypeStruct((slabs, count, columns), jnp.bfloat16),
        in_specs=[pl.BlockSpec(memory_space=pl.ANY) if staged else vmem, vmem],
        out_specs=vmem,
        scratch_shapes=[
            pltpu.SemaphoreType.DMA((2, slabs)),
            pltpu.SemaphoreType.DMA((2, slabs)),
        ]
        + stage,
        compiler_params=pltpu.CompilerParams(
            collective_id=0 if staged else 3, has_side_effects=True, vmem_limit_bytes=VMEM_LIMIT
        ),
        cost_estimate=pl.CostEstimate(
            flops=2 * count * field.shape[0] * columns,
            bytes_accessed=2 * (slabs * count + field.shape[0]) * columns,
            transcendentals=0,
        ),
    )(field, rows)


def pack(starts, gathered, packed):
    slabs, count, _ = gathered.shape
    packed[...] = jnp.zeros_like(packed)

    def one(slot, carry):
        place = pl.ds(pl.multiple_of(starts[slot], ALIGN), count)
        packed[place, :] = packed[place, :] + gathered[slot]
        return carry

    lax.fori_loop(0, slabs, one, 0)


def pack_kernel(with_transpose, starts, gathered, points, *rest):
    packed = rest[-1]
    pack(starts, gathered, packed)
    value = packed[: points.shape[0], :]
    points[...] = value
    if with_transpose:
        rest[0][...] = value.T


def packed_points(starts, gathered, total, with_transpose):
    slabs, count, columns = gathered.shape
    vmem = pl.BlockSpec(memory_space=pltpu.VMEM)
    shapes = [jax.ShapeDtypeStruct((total, columns), jnp.bfloat16)]
    if with_transpose:
        shapes.append(jax.ShapeDtypeStruct((columns, total), jnp.bfloat16))
    return pl.pallas_call(
        functools.partial(pack_kernel, with_transpose),
        out_shape=shapes,
        in_specs=[pl.BlockSpec(memory_space=pltpu.SMEM), vmem],
        out_specs=[vmem] * len(shapes),
        scratch_shapes=[pltpu.VMEM((total + count, columns), jnp.bfloat16)],
        compiler_params=pltpu.CompilerParams(vmem_limit_bytes=VMEM_LIMIT),
    )(starts, gathered)


def apply_kernel(first, n, slabs, *refs):
    if first:
        source, orbitals, table_in, pot, points, points_t, out, kernel_out = refs[:8]
        rest = refs[8:]
    else:
        source, orbitals, table_in, pot, points, field, out = refs[:7]
        rest = refs[7:]
    (orbs, table, insem, kbuf, part, ext, base, sent, got, ksem, osem,
     red_send, red_recv, bc_send, bc_recv, halo_send, halo_recv) = rest
    if first:
        field, prev = orbs, None
    else:
        prev = orbs
    inward = [
        pltpu.make_async_copy(orbitals, orbs, insem.at[0]),
        pltpu.make_async_copy(table_in, table, insem.at[1]),
    ]
    for one in inward:
        one.start()
    z = lax.axis_index("pt")
    s = lax.axis_index("slab")
    cells, columns = out.shape
    half = columns // 2
    chunks = cells // CHUNK
    per_block = BLOCK // CHUNK
    per_plane = PLANE // CHUNK
    rim = WIDTH * PLANE
    scale = 0.25 if first else 0.5
    owners = (n // 2 - 1, n // 2)
    depth = n // 2
    is_owner = (z == owners[0]) | (z == owners[1])
    upper = lax.rem(s + 1, slabs)
    lower = lax.rem(s + slabs - 1, slabs)

    def block_rows(i):
        return pl.ds(pl.multiple_of(i * BLOCK, BLOCK), BLOCK)

    def fetch(i):
        rows = block_rows(i)
        return pltpu.make_async_copy(source.at[rows, :], kbuf.at[rows, :], ksem.at[i])

    def keep(i):
        rows = block_rows(i)
        return pltpu.make_async_copy(kbuf.at[rows, :], kernel_out.at[rows, :], osem.at[i])

    def fetch_start(i, carry):
        fetch(i).start()
        return carry

    lax.fori_loop(0, cells // BLOCK, fetch_start, 0)

    barrier = pltpu.get_barrier_semaphore()

    @pl.when(z > 0)
    def _():
        pl.semaphore_signal(barrier, inc=1, device_id={"pt": z - 1}, device_id_type=MESH)

    @pl.when(z < n - 1)
    def _():
        pl.semaphore_signal(barrier, inc=1, device_id={"pt": z + 1}, device_id_type=MESH)

    @pl.when(is_owner)
    def _():
        pl.semaphore_signal(barrier, inc=1, device_id={"slab": upper}, device_id_type=MESH)
        pl.semaphore_signal(barrier, inc=1, device_id={"slab": lower}, device_id_type=MESH)

    greeted = jnp.where(is_owner, 2, 0) + jnp.where(z > 0, 1, 0) + jnp.where(z < n - 1, 1, 0)
    pl.semaphore_wait(barrier, greeted)

    for one in inward:
        one.wait()

    def halo(k):
        src, dst, to = ((cells, 0, upper), (rim, rim + cells, lower))[k]
        return pltpu.make_async_remote_copy(
            src_ref=ext.at[pl.ds(src, rim), :],
            dst_ref=ext.at[pl.ds(dst, rim), :],
            send_sem=halo_send.at[k],
            recv_sem=halo_recv.at[k],
            device_id={"slab": to},
            device_id_type=MESH,
        )

    own = pl.ds(pl.multiple_of(jnp.where(z == owners[0], 0, half), half), half)

    @pl.when(is_owner)
    def _():
        ext[rim : rim + cells, :] = field[:, own]
        halo(0).start()
        halo(1).start()

    def chunk_rows(c):
        return pl.ds(pl.multiple_of(c * CHUNK, CHUNK), CHUNK)

    def reduce_copy(h, side, c, to):
        rows = chunk_rows(c)
        return pltpu.make_async_remote_copy(
            src_ref=sent.at[h, rows, :],
            dst_ref=got.at[h, side, rows, :],
            send_sem=red_send.at[h, c],
            recv_sem=red_recv.at[h, side, c],
            device_id={"pt": to},
            device_id_type=MESH,
        )

    def result_copy(h, side, c, to):
        view = out.at[chunk_rows(c), pl.ds(h * half, half)]
        return pltpu.make_async_remote_copy(
            src_ref=view,
            dst_ref=view,
            send_sem=bc_send.at[h, side, c],
            recv_sem=bc_recv.at[h, c],
            device_id={"pt": to},
            device_id_type=MESH,
        )

    def local_plane(k):
        def plane(i):
            return ext[pl.ds(pl.multiple_of((k + WIDTH + i) * PLANE, PLANE), PLANE), :]

        rows = pl.ds(pl.multiple_of(k * PLANE, PLANE), PLANE)
        centre = plane(0)
        terms = jnp.dot(table[...], centre, preferred_element_type=jnp.float32)
        summed = terms[:PLANE] + (terms[PLANE : 2 * PLANE] + terms[2 * PLANE :])
        for offset in range(1, WIDTH + 1):
            pair = plane(offset).astype(jnp.float32) + plane(-offset).astype(jnp.float32)
            summed = summed + stencil_coef[offset] * pair
        level = jnp.broadcast_to(pot[pl.ds(k, 1), :], (8, PLANE)).T[:, :1]
        value = scale * (-0.5 * summed + (level - 3.5) * centre.astype(jnp.float32))
        if prev is not None:
            value = value - prev[rows, own].astype(jnp.float32)
        base[rows, :] = value

    def step(t, carry):
        @pl.when((lax.rem(t, per_block) == 0) & (t < chunks))
        def _():
            i = lax.div(t, per_block)
            fetch(i).wait()
            rows = block_rows(i)
            if first:
                density = jnp.dot(
                    field[rows, :], points_t[...], preferred_element_type=jnp.float32
                )
                kbuf[rows, :] = (kbuf[rows, :].astype(jnp.float32) * density).astype(jnp.bfloat16)
                keep(i).start()
            part[rows, :] = jnp.dot(
                kbuf[rows, :], points[...], preferred_element_type=jnp.float32
            )

        o = t - LAG * depth

        @pl.when(is_owner & (o == 0))
        def _():
            halo(0).wait()
            halo(1).wait()

        @pl.when(is_owner & (o >= 0) & (o < chunks) & (lax.rem(o + chunks, per_plane) == 0))
        def _():
            local_plane(lax.div(o, per_plane))

        for h, owner in enumerate(owners):
            cols = pl.ds(h * half, half)

            for side in range(2):
                level = z if side == 0 else n - 1 - z
                inside = (z < owner) if side == 0 else (z > owner)
                back = z - 1 if side == 0 else z + 1
                ahead = z + 1 if side == 0 else z - 1
                c = t - LAG * level

                @pl.when(inside & (c >= 0) & (c < chunks))
                def _():
                    rows = chunk_rows(c)
                    value = part[rows, cols]

                    @pl.when(level == 0)
                    def _():
                        sent[h, rows, :] = value.astype(jnp.bfloat16)

                    @pl.when(level > 0)
                    def _():
                        reduce_copy(h, side, c, back).wait_recv()
                        total = value + got[h, side, rows, :].astype(jnp.float32)
                        sent[h, rows, :] = total.astype(jnp.bfloat16)

                    reduce_copy(h, side, c, ahead).start()

            @pl.when((z == owner) & (o >= 0) & (o < chunks))
            def _():
                rows = chunk_rows(o)
                total = part[rows, cols]
                if owner > 0:
                    reduce_copy(h, 0, o, z - 1).wait_recv()
                    total = total + got[h, 0, rows, :].astype(jnp.float32)
                if owner < n - 1:
                    reduce_copy(h, 1, o, z + 1).wait_recv()
                    total = total + got[h, 1, rows, :].astype(jnp.float32)
                out[rows, cols] = (base[rows, :] - scale * total).astype(jnp.bfloat16)
                if owner > 0:
                    result_copy(h, 0, o, z - 1).start()
                if owner < n - 1:
                    result_copy(h, 1, o, z + 1).start()

            for side in range(2):
                inside = (z < owner) if side == 0 else (z > owner)
                away = owner - z if side == 0 else z - owner
                back = z + 1 if side == 0 else z - 1
                ahead = z - 1 if side == 0 else z + 1
                more = (z > 0) if side == 0 else (z < n - 1)
                b = o - LAG * away

                @pl.when(inside & (b >= 0) & (b < chunks))
                def _():
                    result_copy(h, side, b, back).wait_recv()

                    @pl.when(more)
                    def _():
                        result_copy(h, side, b, ahead).start()

        return carry

    lax.fori_loop(0, chunks + 2 * LAG * depth, step, 0)

    def finish(c, carry):
        for h, owner in enumerate(owners):
            @pl.when(z < owner)
            def _():
                reduce_copy(h, 0, c, z + 1).wait_send()

            @pl.when(z > owner)
            def _():
                reduce_copy(h, 1, c, z - 1).wait_send()

            @pl.when((z <= owner) & (z > 0))
            def _():
                result_copy(h, 0, c, z - 1).wait_send()

            @pl.when((z >= owner) & (z < n - 1))
            def _():
                result_copy(h, 1, c, z + 1).wait_send()

        return carry

    lax.fori_loop(0, chunks, finish, 0)
    if first:
        def kept(i, carry):
            keep(i).wait()
            return carry

        lax.fori_loop(0, cells // BLOCK, kept, 0)


def apply_turn(first, n, slabs, source, operands):
    cells, total = source.shape
    columns = operands[0].shape[1]
    table = operands[1]
    half = columns // 2
    chunks = cells // CHUNK
    blocks = cells // BLOCK
    vmem = pl.BlockSpec(memory_space=pltpu.VMEM)
    anywhere = pl.BlockSpec(memory_space=pl.ANY)
    shapes = [jax.ShapeDtypeStruct((cells, columns), jnp.bfloat16)]
    if first:
        shapes.append(jax.ShapeDtypeStruct((cells, total), jnp.bfloat16))
    return pl.pallas_call(
        functools.partial(apply_kernel, first, n, slabs),
        out_shape=shapes,
        in_specs=[anywhere] * 3 + [vmem] * (len(operands) - 2),
        out_specs=[vmem, anywhere][: len(shapes)],
        scratch_shapes=[
            pltpu.VMEM((cells, columns), jnp.bfloat16),
            pltpu.VMEM(table.shape, table.dtype),
            pltpu.SemaphoreType.DMA((2,)),
            pltpu.VMEM((cells, total), jnp.bfloat16),
            pltpu.VMEM((cells, columns), jnp.float32),
            pltpu.VMEM((cells + 2 * WIDTH * PLANE, half), jnp.bfloat16),
            pltpu.VMEM((cells, half), jnp.float32),
            pltpu.VMEM((2, cells, half), jnp.bfloat16),
            pltpu.VMEM((2, 2, cells, half), jnp.bfloat16),
            pltpu.SemaphoreType.DMA((blocks,)),
            pltpu.SemaphoreType.DMA((blocks,)),
            pltpu.SemaphoreType.DMA((2, chunks)),
            pltpu.SemaphoreType.DMA((2, 2, chunks)),
            pltpu.SemaphoreType.DMA((2, 2, chunks)),
            pltpu.SemaphoreType.DMA((2, chunks)),
            pltpu.SemaphoreType.DMA((2,)),
            pltpu.SemaphoreType.DMA((2,)),
        ],
        compiler_params=pltpu.CompilerParams(
            collective_id=1 if first else 2, has_side_effects=True, vmem_limit_bytes=VMEM_LIMIT
        ),
        cost_estimate=pl.CostEstimate(
            flops=2 * cells * total * columns, bytes_accessed=2 * cells * total, transcendentals=0
        ),
    )(source, *operands)


def rows_kernel(counts, listed, rows, starts, wide):
    z = lax.axis_index("pt")
    me = lax.axis_index("slab")
    slabs = counts.shape[1]
    capacity = listed.shape[2]

    def one(s, carry):
        place, mine = carry
        starts[lax.bitwise_xor(s, me)] = lax.div(place, ALIGN) * ALIGN
        mine = jnp.where(s == me, place, mine)
        return place + counts[z, s], mine

    _, mine = lax.fori_loop(0, slabs, one, (jnp.int32(0), jnp.int32(0)))
    lane = lax.broadcasted_iota(jnp.int32, (8, capacity), 1)
    value = jnp.broadcast_to(listed[z], (8, capacity))
    wide[...] = jnp.full(wide.shape, -1.0, jnp.float32)
    wide[:, :capacity] = jnp.where(lane < counts[z, me], value, -1).astype(jnp.float32)
    moved = pltpu.roll(wide[...], lax.rem(mine, ALIGN), 1)
    rows[...] = moved.T[: rows.shape[0], :1].astype(jnp.int32)


def shifted_rows(owner_rows, owner_count):
    slabs = owner_count.shape[1]
    count = owner_rows.shape[2] + ALIGN
    width = (count + 127) // 128 * 128
    smem = pl.BlockSpec(memory_space=pltpu.SMEM)
    vmem = pl.BlockSpec(memory_space=pltpu.VMEM)
    return pl.pallas_call(
        rows_kernel,
        out_shape=[
            jax.ShapeDtypeStruct((count, 1), jnp.int32),
            jax.ShapeDtypeStruct((slabs,), jnp.int32),
        ],
        in_specs=[smem, vmem],
        out_specs=[vmem, smem],
        scratch_shapes=[pltpu.VMEM((8, width), jnp.float32)],
    )(owner_count, owner_rows)


def body(n, slabs, orbitals, potential, fit_matrix, owner_rows, owner_count):
    rows, starts = shifted_rows(owner_rows, owner_count)
    pot = potential.reshape(-1, PLANE)
    table = jnp.asarray(plane_table())
    total = fit_matrix.shape[1]
    gathered = gather_points(orbitals, rows, slabs, True)
    points, points_t = packed_points(starts, gathered, total, True)
    current, kernel = apply_turn(
        True, n, slabs, fit_matrix, (orbitals, table, pot, points, points_t)
    )
    previous = orbitals
    for _ in range(1, DEG):
        gathered = gather_points(current, rows, slabs, False)
        (points,) = packed_points(starts, gathered, total, False)
        (upcoming,) = apply_turn(
            False, n, slabs, kernel, (previous, table, pot, points, current)
        )
        previous, current = current, upcoming
    return current


def solution(mesh):
    placed = (P("slab", None), P("slab"), P("slab", "pt"), P(None, "slab", None), P())
    return jax.shard_map(
        functools.partial(body, mesh.shape["pt"], mesh.shape["slab"]),
        mesh=mesh, in_specs=placed, out_specs=P("slab", None), check_vma=False,
    )
```

```python
import functools

import jax
import jax.numpy as jnp
import ml_dtypes
import numpy as np
from jax import lax
from jax.experimental import pallas as pl
from jax.experimental.pallas import tpu as pltpu
from jax.sharding import PartitionSpec as P

NY = 8
NX = 32
PLANE = NY * NX
WIDTH = 4
ALIGN = 16
MESH = pl.DeviceIdType.MESH
VMEM_LIMIT = 56 * 1024 * 1024
BLOCK = 256
CHUNK = 128
LAG = 4
PAD = 128

stencil_coef = (-205.0 / 72.0, 8.0 / 5.0, -1.0 / 5.0, 8.0 / 315.0, -1.0 / 560.0)


def plane_table():
    cells = np.arange(PLANE)
    row_y, col_x = cells // NX, cells % NX
    diff_y = (row_y[:, None] - row_y[None, :]) % NY
    diff_x = (col_x[:, None] - col_x[None, :]) % NX
    same_y, same_x = diff_y == 0, diff_x == 0
    table = np.where(same_y & same_x, 3.0 * stencil_coef[0], 0.0)
    for offset in range(1, WIDTH + 1):
        for shift in (offset, -offset):
            table = table + stencil_coef[offset] * (same_y & (diff_x == shift % NX))
            table = table + stencil_coef[offset] * (same_x & (diff_y == shift % NY))
    terms, rest = [], table.astype(np.float32)
    for _ in range(3):
        term = rest.astype(ml_dtypes.bfloat16)
        terms.append(term)
        rest = rest - term.astype(np.float32)
    return np.concatenate(terms, axis=0)


def flipped(index, bit):
    size = 1 << bit
    return index + size - 2 * size * lax.rem(lax.div(index, size), 2)


def filter_kernel(
    n, slabs, fit, orbitals, table_in, pot, rows, places, out,
    orbs, table, kbuf, chosen, all_points, points_a, points_b, points, points_t, fields, first_field,
    part, ext, base, sent, got,
    insem, ksem, ag_send, ag_recv, red_send, red_recv, bc_send, bc_recv, halo_send, halo_recv,
):
    z = lax.axis_index("pt")
    s = lax.axis_index("slab")
    cells, columns = out.shape
    half = columns // 2
    total = kbuf.shape[1]
    count = rows.shape[0]
    bits = slabs.bit_length() - 1
    chunks = cells // CHUNK
    blocks = cells // BLOCK
    per_block = BLOCK // CHUNK
    per_plane = PLANE // CHUNK
    rim = WIDTH * PLANE
    owners = (n // 2 - 1, n // 2)
    depth = n // 2
    is_owner = (z == owners[0]) | (z == owners[1])
    upper = lax.rem(s + 1, slabs)
    lower = lax.rem(s + slabs - 1, slabs)
    results = (first_field, out)
    span = chunks + 2 * LAG * depth
    turn_two = chunks + span
    begins = ((0, chunks), (turn_two, turn_two + chunks))

    inward = [
        pltpu.make_async_copy(orbitals, orbs, insem.at[0]),
        pltpu.make_async_copy(table_in, table, insem.at[1]),
    ]
    for one in inward:
        one.start()

    def block_rows(i):
        return pl.ds(pl.multiple_of(i * BLOCK, BLOCK), BLOCK)

    def chunk_rows(c):
        return pl.ds(pl.multiple_of(c * CHUNK, CHUNK), CHUNK)

    def fetch(i):
        return pltpu.make_async_copy(
            fit.at[block_rows(i), :], kbuf.at[block_rows(i), :], ksem.at[i]
        )

    def fetch_start(i, carry):
        fetch(i).start()
        return carry

    lax.fori_loop(0, blocks, fetch_start, 0)

    barrier = pltpu.get_barrier_semaphore()
    for bit in range(bits):
        pl.semaphore_signal(
            barrier, inc=1, device_id={"slab": flipped(s, bit)}, device_id_type=MESH
        )

    @pl.when(z > 0)
    def _():
        pl.semaphore_signal(barrier, inc=1, device_id={"pt": z - 1}, device_id_type=MESH)

    @pl.when(z < n - 1)
    def _():
        pl.semaphore_signal(barrier, inc=1, device_id={"pt": z + 1}, device_id_type=MESH)

    @pl.when(is_owner)
    def _():
        pl.semaphore_signal(barrier, inc=1, device_id={"slab": upper}, device_id_type=MESH)
        pl.semaphore_signal(barrier, inc=1, device_id={"slab": lower}, device_id_type=MESH)

    for slot in range(slabs):
        all_points[slot, :PAD, :] = jnp.zeros((PAD, columns), jnp.bfloat16)
        all_points[slot, PAD + count :, :] = jnp.zeros((PAD, columns), jnp.bfloat16)
        for side_points in (points_a, points_b):
            side_points[slot, :PAD, :] = jnp.zeros((PAD, half), jnp.bfloat16)
            side_points[slot, PAD + count :, :] = jnp.zeros((PAD, half), jnp.bfloat16)

    cell_ids = lax.broadcasted_iota(jnp.int32, (count, cells), 1)
    chosen[...] = jnp.where(rows[...] == cell_ids, 1.0, 0.0).astype(jnp.bfloat16)
    for one in inward:
        one.wait()

    gathers = (all_points, points_a, points_b)
    cut = (count // 2 + ALIGN - 1) // ALIGN * ALIGN
    pieces = ((0, cut), (cut, count - cut))
    outer = list(range(1, bits))
    orders = (outer + [0], outer[::-1] + [0])
    tree = []
    for piece in range(2):
        for slot in range(1, slabs):
            place = max(i for i in range(bits) if slot >> orders[piece][i] & 1)
            tree.append((bin(slot).count("1"), piece, slot, place))
    tree.sort()

    def gather_copy(g, piece, target, place):
        bit = orders[piece][place]
        begin, size = pieces[piece]
        view = gathers[g]
        return pltpu.make_async_remote_copy(
            src_ref=view.at[target ^ (1 << bit), pl.ds(PAD + begin, size), :],
            dst_ref=view.at[target, pl.ds(PAD + begin, size), :],
            send_sem=ag_send.at[g, piece, target],
            recv_sem=ag_recv.at[g, piece, target],
            device_id={"slab": flipped(s, bit)},
            device_id_type=MESH,
        )

    def gather_start(g, field):
        picked = jnp.dot(chosen[...], field, preferred_element_type=jnp.float32)
        gathers[g][0, PAD : PAD + count, :] = picked.astype(jnp.bfloat16)

    def gather_send(g):
        for place in range(bits):
            for piece in range(2):
                gather_copy(g, piece, 1 << orders[piece][place], place).start()

    def gather_forward(g, level):
        for hops, piece, slot, place in tree:
            if hops == level and place < bits - 1:
                gather_copy(g, piece, slot, place).wait_recv()
                for later in range(place + 1, bits):
                    gather_copy(g, piece, slot | (1 << orders[piece][later]), later).start()

    def gather_end(g):
        for _, piece, slot, place in tree:
            if place == bits - 1:
                gather_copy(g, piece, slot, place).wait_recv()

    def gather_sent(g):
        for _, piece, slot, place in tree:
            gather_copy(g, piece, slot, place).wait_send()

    def pack(g, keep):
        width = total // PAD

        def one(b, carry):
            value = None
            for slot in range(slabs):
                begin = places[slot * width + b] * ALIGN
                run = gathers[g][slot, pl.ds(begin, PAD), :]
                value = run if value is None else value + run
            keep(pl.ds(pl.multiple_of(b * PAD, PAD), PAD), value)
            return carry

        lax.fori_loop(0, width, one, 0)

    gather_start(0, orbs[...])
    greeted = jnp.where(is_owner, 2, 0) + jnp.where(z > 0, 1, 0) + jnp.where(z < n - 1, 1, 0)
    pl.semaphore_wait(barrier, greeted + bits)
    gather_send(0)

    def halo(turn, k):
        src, dst, to = ((cells, 0, upper), (rim, rim + cells, lower))[k]
        return pltpu.make_async_remote_copy(
            src_ref=ext.at[turn, pl.ds(src, rim), :],
            dst_ref=ext.at[turn, pl.ds(dst, rim), :],
            send_sem=halo_send.at[turn, k],
            recv_sem=halo_recv.at[turn, k],
            device_id={"slab": to},
            device_id_type=MESH,
        )

    for h, owner in enumerate(owners):
        @pl.when(z == owner)
        def _():
            ext[0, rim : rim + cells, :] = orbs[:, h * half : (h + 1) * half]

    for level in range(1, bits):
        gather_forward(0, level)

    @pl.when(is_owner)
    def _():
        halo(0, 0).start()
        halo(0, 1).start()

    gather_end(0)

    def keep_all(place, value):
        points[place, :] = value
        points_t[:, place] = value.T

    pack(0, keep_all)

    def reduce_copy(turn, h, side, c, to):
        return pltpu.make_async_remote_copy(
            src_ref=sent.at[turn, h, chunk_rows(c), :],
            dst_ref=got.at[turn, h, side, chunk_rows(c), :],
            send_sem=red_send.at[turn, h, c],
            recv_sem=red_recv.at[turn, h, side, c],
            device_id={"pt": to},
            device_id_type=MESH,
        )

    def result_copy(turn, h, side, c, to):
        view = results[turn].at[chunk_rows(c), pl.ds(h * half, half)]
        return pltpu.make_async_remote_copy(
            src_ref=view,
            dst_ref=view,
            send_sem=bc_send.at[turn, h, side, c],
            recv_sem=bc_recv.at[turn, h, c],
            device_id={"pt": to},
            device_id_type=MESH,
        )

    def local_plane(turn, h, k):
        def plane(i):
            return ext[turn, pl.ds(pl.multiple_of((k + WIDTH + i) * PLANE, PLANE), PLANE), :]

        place = pl.ds(pl.multiple_of(k * PLANE, PLANE), PLANE)
        scale = 0.5 if turn else 0.25
        centre = plane(0)
        terms = jnp.dot(table[...], centre, preferred_element_type=jnp.float32)
        summed = terms[:PLANE] + (terms[PLANE : 2 * PLANE] + terms[2 * PLANE :])
        for offset in range(1, WIDTH + 1):
            pair = plane(offset).astype(jnp.float32) + plane(-offset).astype(jnp.float32)
            summed = summed + stencil_coef[offset] * pair
        level = jnp.broadcast_to(pot[pl.ds(k, 1), :], (8, PLANE)).T[:, :1]
        value = scale * (-0.5 * summed + (level - 3.5) * centre.astype(jnp.float32))
        if turn:
            value = value - orbs[place, h * half : (h + 1) * half].astype(jnp.float32)
        base[place, :] = value

    def stream(turn, h, t):
        owner = owners[h]
        scale = 0.5 if turn else 0.25
        cols = pl.ds(h * half, half)
        u = t - begins[turn][h]
        o = u - LAG * depth

        for side in range(2):
            level = z if side == 0 else n - 1 - z
            inside = (z < owner) if side == 0 else (z > owner)
            back = z - 1 if side == 0 else z + 1
            ahead = z + 1 if side == 0 else z - 1
            c = u - LAG * level

            @pl.when(inside & (c >= 0) & (c < chunks))
            def _():
                place = chunk_rows(c)
                value = part[place, cols]

                @pl.when(level == 0)
                def _():
                    sent[turn, h, place, :] = value.astype(jnp.bfloat16)

                @pl.when(level > 0)
                def _():
                    reduce_copy(turn, h, side, c, back).wait_recv()
                    summed = value + got[turn, h, side, place, :].astype(jnp.float32)
                    sent[turn, h, place, :] = summed.astype(jnp.bfloat16)

                reduce_copy(turn, h, side, c, ahead).start()

        @pl.when((z == owner) & (o >= 0) & (o < chunks))
        def _():
            @pl.when(o == 0)
            def _():
                halo(turn, 0).wait()
                halo(turn, 1).wait()

            @pl.when(lax.rem(o, per_plane) == 0)
            def _():
                local_plane(turn, h, lax.div(o, per_plane))

            place = chunk_rows(o)
            summed = part[place, cols]
            if owner > 0:
                reduce_copy(turn, h, 0, o, z - 1).wait_recv()
                summed = summed + got[turn, h, 0, place, :].astype(jnp.float32)
            if owner < n - 1:
                reduce_copy(turn, h, 1, o, z + 1).wait_recv()
                summed = summed + got[turn, h, 1, place, :].astype(jnp.float32)
            value = (base[place, :] - scale * summed).astype(jnp.bfloat16)
            results[turn][place, cols] = value
            if owner > 0:
                result_copy(turn, h, 0, o, z - 1).start()
            if owner < n - 1:
                result_copy(turn, h, 1, o, z + 1).start()
            if turn == 0:
                ext[1, pl.ds(pl.multiple_of(rim + o * CHUNK, CHUNK), CHUNK), :] = value

                @pl.when(o == chunks - 1)
                def _():
                    halo(1, 0).start()
                    halo(1, 1).start()

        for side in range(2):
            inside = (z < owner) if side == 0 else (z > owner)
            away = owner - z if side == 0 else z - owner
            back = z + 1 if side == 0 else z - 1
            ahead = z - 1 if side == 0 else z + 1
            more = (z > 0) if side == 0 else (z < n - 1)
            b = o - LAG * away

            @pl.when(inside & (b >= 0) & (b < chunks))
            def _():
                result_copy(turn, h, side, b, back).wait_recv()

                @pl.when(more)
                def _():
                    result_copy(turn, h, side, b, ahead).start()

    def gather_half(h, t):
        ready = begins[0][h] + span
        gap = chunks // (bits + 1)
        g = 1 + h

        @pl.when(t == ready)
        def _():
            gather_start(g, first_field[:, h * half : (h + 1) * half])
            gather_send(g)

        for level in range(1, bits):
            @pl.when(t == ready + level * gap)
            def _():
                gather_forward(g, level)

        @pl.when(t == ready + chunks - 1)
        def _():
            gather_end(g)

            def keep_half(place, value):
                fields[h, place, :] = value

            pack(g, keep_half)

    def first_turn(t, carry):
        @pl.when((lax.rem(t, per_block) == 0) & (t < chunks))
        def _():
            i = lax.div(t, per_block)
            fetch(i).wait()
            place = block_rows(i)
            density = jnp.dot(orbs[place, :], points_t[...], preferred_element_type=jnp.float32)
            kbuf[place, :] = (kbuf[place, :].astype(jnp.float32) * density).astype(jnp.bfloat16)
            part[place, :] = jnp.dot(
                kbuf[place, :], points[...], preferred_element_type=jnp.float32
            )

        stream(0, 0, t)
        stream(0, 1, t)
        gather_half(0, t)
        return carry

    lax.fori_loop(0, turn_two, first_turn, 0)

    def second_turn(t, carry):
        for h in range(2):
            u = t - begins[1][h]

            @pl.when((u >= 0) & (u < chunks) & (lax.rem(t, per_block) == 0))
            def _():
                place = block_rows(lax.div(u, per_block))
                part[place, h * half : (h + 1) * half] = jnp.dot(
                    kbuf[place, :], fields[h], preferred_element_type=jnp.float32
                )

        stream(1, 0, t)
        stream(1, 1, t)
        gather_half(1, t)
        return carry

    lax.fori_loop(turn_two, turn_two + chunks + span, second_turn, 0)

    def finish(c, carry):
        for turn in range(2):
            for h, owner in enumerate(owners):
                @pl.when(z < owner)
                def _():
                    reduce_copy(turn, h, 0, c, z + 1).wait_send()

                @pl.when(z > owner)
                def _():
                    reduce_copy(turn, h, 1, c, z - 1).wait_send()

                @pl.when((z <= owner) & (z > 0))
                def _():
                    result_copy(turn, h, 0, c, z - 1).wait_send()

                @pl.when((z >= owner) & (z < n - 1))
                def _():
                    result_copy(turn, h, 1, c, z + 1).wait_send()

        return carry

    lax.fori_loop(0, chunks, finish, 0)
    for g in range(3):
        gather_sent(g)


def filtered(n, slabs, fit, orbitals, table, pot, rows, places):
    cells, total = fit.shape
    columns = orbitals.shape[1]
    half = columns // 2
    count = rows.shape[0]
    chunks = cells // CHUNK
    vmem = pl.BlockSpec(memory_space=pltpu.VMEM)
    anywhere = pl.BlockSpec(memory_space=pl.ANY)
    bf16, f32, dma = jnp.bfloat16, jnp.float32, pltpu.SemaphoreType.DMA
    return pl.pallas_call(
        functools.partial(filter_kernel, n, slabs),
        out_shape=jax.ShapeDtypeStruct((cells, columns), bf16),
        in_specs=[anywhere] * 3 + [vmem, vmem, pl.BlockSpec(memory_space=pltpu.SMEM)],
        out_specs=vmem,
        scratch_shapes=[
            pltpu.VMEM((cells, columns), bf16),
            pltpu.VMEM(table.shape, bf16),
            pltpu.VMEM((cells, total), bf16),
            pltpu.VMEM((count, cells), bf16),
            pltpu.VMEM((slabs, count + 2 * PAD, columns), bf16),
            pltpu.VMEM((slabs, count + 2 * PAD, half), bf16),
            pltpu.VMEM((slabs, count + 2 * PAD, half), bf16),
            pltpu.VMEM((total, columns), bf16),
            pltpu.VMEM((columns, total), bf16),
            pltpu.VMEM((2, total, half), bf16),
            pltpu.VMEM((cells, columns), bf16),
            pltpu.VMEM((cells, columns), f32),
            pltpu.VMEM((2, cells + 2 * WIDTH * PLANE, half), bf16),
            pltpu.VMEM((cells, half), f32),
            pltpu.VMEM((2, 2, cells, half), bf16),
            pltpu.VMEM((2, 2, 2, cells, half), bf16),
            dma((2,)),
            dma((cells // BLOCK,)),
            dma((3, 2, slabs)),
            dma((3, 2, slabs)),
            dma((2, 2, chunks)),
            dma((2, 2, 2, chunks)),
            dma((2, 2, 2, chunks)),
            dma((2, 2, chunks)),
            dma((2, 2)),
            dma((2, 2)),
        ],
        compiler_params=pltpu.CompilerParams(
            collective_id=0, has_side_effects=True, vmem_limit_bytes=VMEM_LIMIT
        ),
        cost_estimate=pl.CostEstimate(
            flops=6 * cells * total * columns, bytes_accessed=2 * cells * total, transcendentals=0
        ),
    )(fit, orbitals, table, pot, rows, places)


def rows_kernel(counts, listed, rows, places, wide):
    z = lax.axis_index("pt")
    me = lax.axis_index("slab")
    slabs = counts.shape[1]
    capacity = listed.shape[2]
    count = rows.shape[0]
    width = places.shape[0] // slabs

    def one(s, carry):
        place, mine = carry
        start = lax.div(place, ALIGN) * ALIGN
        slot = lax.bitwise_xor(s, me)

        def block(b, inner):
            places[slot * width + b] = lax.div(
                jnp.clip(b * PAD - start + PAD, 0, PAD + count), ALIGN
            )
            return inner

        lax.fori_loop(0, width, block, 0)
        mine = jnp.where(s == me, place, mine)
        return place + counts[z, s], mine

    _, mine = lax.fori_loop(0, slabs, one, (jnp.int32(0), jnp.int32(0)))
    lane = lax.broadcasted_iota(jnp.int32, (8, capacity), 1)
    value = jnp.broadcast_to(listed[z], (8, capacity))
    wide[...] = jnp.full(wide.shape, -1.0, jnp.float32)
    wide[:, :capacity] = jnp.where(lane < counts[z, me], value, -1).astype(jnp.float32)
    moved = pltpu.roll(wide[...], lax.rem(mine, ALIGN), 1)
    rows[...] = moved.T[:count, :1].astype(jnp.int32)


def shifted_rows(owner_rows, owner_count, total):
    slabs = owner_count.shape[1]
    count = owner_rows.shape[2] + ALIGN
    lanes = (count + 127) // 128 * 128
    smem = pl.BlockSpec(memory_space=pltpu.SMEM)
    vmem = pl.BlockSpec(memory_space=pltpu.VMEM)
    return pl.pallas_call(
        rows_kernel,
        out_shape=[
            jax.ShapeDtypeStruct((count, 1), jnp.int32),
            jax.ShapeDtypeStruct((slabs * (total // PAD),), jnp.int32),
        ],
        in_specs=[smem, vmem],
        out_specs=[vmem, smem],
        scratch_shapes=[pltpu.VMEM((8, lanes), jnp.float32)],
    )(owner_count, owner_rows)


def body(n, slabs, orbitals, potential, fit_matrix, owner_rows, owner_count):
    rows, places = shifted_rows(owner_rows, owner_count, fit_matrix.shape[1])
    pot = potential.reshape(-1, PLANE)
    table = jnp.asarray(plane_table())
    return filtered(n, slabs, fit_matrix, orbitals, table, pot, rows, places)


def solution(mesh):
    placed = (P("slab", None), P("slab"), P("slab", "pt"), P(None, "slab", None), P())
    return jax.shard_map(
        functools.partial(body, mesh.shape["pt"], mesh.shape["slab"]),
        mesh=mesh, in_specs=placed, out_specs=P("slab", None), check_vma=False,
    )
```

```python
import functools

import jax
import jax.numpy as jnp
import ml_dtypes
import numpy as np
from jax import lax
from jax.experimental import pallas as pl
from jax.experimental.pallas import tpu as pltpu
from jax.sharding import PartitionSpec as P

NY = 8
NX = 32
PLANE = NY * NX
WIDTH = 4
ALIGN = 16
MESH = pl.DeviceIdType.MESH
VMEM_LIMIT = 56 * 1024 * 1024
BLOCK = 256
CHUNK = 128
LAG = 6
PAD = 128

stencil_coef = (-205.0 / 72.0, 8.0 / 5.0, -1.0 / 5.0, 8.0 / 315.0, -1.0 / 560.0)


def plane_table():
    cells = np.arange(PLANE)
    row_y, col_x = cells // NX, cells % NX
    diff_y = (row_y[:, None] - row_y[None, :]) % NY
    diff_x = (col_x[:, None] - col_x[None, :]) % NX
    same_y, same_x = diff_y == 0, diff_x == 0
    table = np.where(same_y & same_x, 3.0 * stencil_coef[0], 0.0)
    for offset in range(1, WIDTH + 1):
        for shift in (offset, -offset):
            table = table + stencil_coef[offset] * (same_y & (diff_x == shift % NX))
            table = table + stencil_coef[offset] * (same_x & (diff_y == shift % NY))
    terms, rest = [], table.astype(np.float32)
    for _ in range(3):
        term = rest.astype(ml_dtypes.bfloat16)
        terms.append(term)
        rest = rest - term.astype(np.float32)
    return np.concatenate(terms, axis=0)


def flipped(index, bit):
    size = 1 << bit
    return index + size - 2 * size * lax.rem(lax.div(index, size), 2)


def filter_kernel(
    n, slabs, fit, orbitals, table_in, pot, rows, places, out,
    orbs, table, kbuf, chosen, all_points, points_a, points_b, points, points_t, fields, first_field,
    part, ext, base, sent, got,
    insem, ksem, ag_send, ag_recv, red_send, red_recv, bc_send, bc_recv, halo_send, halo_recv,
):
    z = lax.axis_index("pt")
    s = lax.axis_index("slab")
    cells, columns = out.shape
    half = columns // 2
    total = kbuf.shape[1]
    count = rows.shape[0]
    bits = slabs.bit_length() - 1
    chunks = cells // CHUNK
    blocks = cells // BLOCK
    per_block = BLOCK // CHUNK
    per_plane = PLANE // CHUNK
    rim = WIDTH * PLANE
    owners = (n // 2 - 1, n // 2)
    depth = n // 2
    is_owner = (z == owners[0]) | (z == owners[1])
    upper = lax.rem(s + 1, slabs)
    lower = lax.rem(s + slabs - 1, slabs)
    results = (first_field, out)
    span = chunks + 2 * LAG * depth
    turn_two = chunks + span
    begins = ((0, chunks), (turn_two, turn_two + chunks))

    inward = [
        pltpu.make_async_copy(orbitals, orbs, insem.at[0]),
        pltpu.make_async_copy(table_in, table, insem.at[1]),
    ]
    for one in inward:
        one.start()

    def block_rows(i):
        return pl.ds(pl.multiple_of(i * BLOCK, BLOCK), BLOCK)

    def chunk_rows(c):
        return pl.ds(pl.multiple_of(c * CHUNK, CHUNK), CHUNK)

    def fetch(i):
        return pltpu.make_async_copy(
            fit.at[block_rows(i), :], kbuf.at[block_rows(i), :], ksem.at[i]
        )

    def fetch_start(i, carry):
        fetch(i).start()
        return carry

    lax.fori_loop(0, blocks, fetch_start, 0)

    barrier = pltpu.get_barrier_semaphore()
    for bit in range(bits):
        pl.semaphore_signal(
            barrier, inc=1, device_id={"slab": flipped(s, bit)}, device_id_type=MESH
        )

    @pl.when(z > 0)
    def _():
        pl.semaphore_signal(barrier, inc=1, device_id={"pt": z - 1}, device_id_type=MESH)

    @pl.when(z < n - 1)
    def _():
        pl.semaphore_signal(barrier, inc=1, device_id={"pt": z + 1}, device_id_type=MESH)

    @pl.when(is_owner)
    def _():
        pl.semaphore_signal(barrier, inc=1, device_id={"slab": upper}, device_id_type=MESH)
        pl.semaphore_signal(barrier, inc=1, device_id={"slab": lower}, device_id_type=MESH)

    for slot in range(slabs):
        all_points[slot, :PAD, :] = jnp.zeros((PAD, columns), jnp.bfloat16)
        all_points[slot, PAD + count :, :] = jnp.zeros((PAD, columns), jnp.bfloat16)
        for side_points in (points_a, points_b):
            side_points[slot, :PAD, :] = jnp.zeros((PAD, half), jnp.bfloat16)
            side_points[slot, PAD + count :, :] = jnp.zeros((PAD, half), jnp.bfloat16)

    cell_ids = lax.broadcasted_iota(jnp.int32, (count, cells), 1)
    chosen[...] = jnp.where(rows[...] == cell_ids, 1.0, 0.0).astype(jnp.bfloat16)
    for one in inward:
        one.wait()

    gathers = (all_points, points_a, points_b)
    cut = (count // 2 + ALIGN - 1) // ALIGN * ALIGN
    pieces = ((0, cut), (cut, count - cut))
    outer = list(range(1, bits))
    orders = (outer + [0], outer[::-1] + [0])
    tree = []
    for piece in range(2):
        for slot in range(1, slabs):
            place = max(i for i in range(bits) if slot >> orders[piece][i] & 1)
            tree.append((bin(slot).count("1"), piece, slot, place))
    tree.sort()

    def gather_copy(g, piece, target, place):
        bit = orders[piece][place]
        begin, size = pieces[piece]
        view = gathers[g]
        return pltpu.make_async_remote_copy(
            src_ref=view.at[target ^ (1 << bit), pl.ds(PAD + begin, size), :],
            dst_ref=view.at[target, pl.ds(PAD + begin, size), :],
            send_sem=ag_send.at[g, piece, target],
            recv_sem=ag_recv.at[g, piece, target],
            device_id={"slab": flipped(s, bit)},
            device_id_type=MESH,
        )

    def gather_start(g, field):
        picked = jnp.dot(chosen[...], field, preferred_element_type=jnp.float32)
        gathers[g][0, PAD : PAD + count, :] = picked.astype(jnp.bfloat16)

    def gather_send(g):
        for place in range(bits):
            for piece in range(2):
                gather_copy(g, piece, 1 << orders[piece][place], place).start()

    def gather_forward(g, level):
        for hops, piece, slot, place in tree:
            if hops == level and place < bits - 1:
                gather_copy(g, piece, slot, place).wait_recv()
                for later in range(place + 1, bits):
                    gather_copy(g, piece, slot | (1 << orders[piece][later]), later).start()

    def gather_end(g):
        for _, piece, slot, place in tree:
            if place == bits - 1:
                gather_copy(g, piece, slot, place).wait_recv()

    def gather_sent(g):
        for _, piece, slot, place in tree:
            gather_copy(g, piece, slot, place).wait_send()

    def pack(g, keep):
        width = total // PAD

        def one(b, carry):
            value = None
            for slot in range(slabs):
                begin = places[slot * width + b] * ALIGN
                run = gathers[g][slot, pl.ds(begin, PAD), :]
                value = run if value is None else value + run
            keep(pl.ds(pl.multiple_of(b * PAD, PAD), PAD), value)
            return carry

        lax.fori_loop(0, width, one, 0)

    gather_start(0, orbs[...])
    greeted = jnp.where(is_owner, 2, 0) + jnp.where(z > 0, 1, 0) + jnp.where(z < n - 1, 1, 0)
    pl.semaphore_wait(barrier, greeted + bits)
    gather_send(0)

    def halo(turn, k):
        src, dst, to = ((cells, 0, upper), (rim, rim + cells, lower))[k]
        return pltpu.make_async_remote_copy(
            src_ref=ext.at[turn, pl.ds(src, rim), :],
            dst_ref=ext.at[turn, pl.ds(dst, rim), :],
            send_sem=halo_send.at[turn, k],
            recv_sem=halo_recv.at[turn, k],
            device_id={"slab": to},
            device_id_type=MESH,
        )

    for h, owner in enumerate(owners):
        @pl.when(z == owner)
        def _():
            ext[0, rim : rim + cells, :] = orbs[:, h * half : (h + 1) * half]

    for level in range(1, bits):
        gather_forward(0, level)

    @pl.when(is_owner)
    def _():
        halo(0, 0).start()
        halo(0, 1).start()

    gather_end(0)

    def keep_all(place, value):
        points[place, :] = value
        points_t[:, place] = value.T

    pack(0, keep_all)

    def reduce_copy(turn, h, side, c, to):
        return pltpu.make_async_remote_copy(
            src_ref=sent.at[turn, h, chunk_rows(c), :],
            dst_ref=got.at[turn, h, side, chunk_rows(c), :],
            send_sem=red_send.at[turn, h, c],
            recv_sem=red_recv.at[turn, h, side, c],
            device_id={"pt": to},
            device_id_type=MESH,
        )

    def result_copy(turn, h, side, c, to):
        view = results[turn].at[chunk_rows(c), pl.ds(h * half, half)]
        return pltpu.make_async_remote_copy(
            src_ref=view,
            dst_ref=view,
            send_sem=bc_send.at[turn, h, side, c],
            recv_sem=bc_recv.at[turn, h, c],
            device_id={"pt": to},
            device_id_type=MESH,
        )

    def local_plane(turn, h, k):
        def plane(i):
            return ext[turn, pl.ds(pl.multiple_of((k + WIDTH + i) * PLANE, PLANE), PLANE), :]

        place = pl.ds(pl.multiple_of(k * PLANE, PLANE), PLANE)
        scale = 0.5 if turn else 0.25
        centre = plane(0)
        terms = jnp.dot(table[...], centre, preferred_element_type=jnp.float32)
        summed = terms[:PLANE] + (terms[PLANE : 2 * PLANE] + terms[2 * PLANE :])
        for offset in range(1, WIDTH + 1):
            pair = plane(offset).astype(jnp.float32) + plane(-offset).astype(jnp.float32)
            summed = summed + stencil_coef[offset] * pair
        level = jnp.broadcast_to(pot[pl.ds(k, 1), :], (8, PLANE)).T[:, :1]
        value = scale * (-0.5 * summed + (level - 3.5) * centre.astype(jnp.float32))
        if turn:
            value = value - orbs[place, h * half : (h + 1) * half].astype(jnp.float32)
        base[place, :] = value

    def stream(turn, h, t):
        owner = owners[h]
        scale = 0.5 if turn else 0.25
        cols = pl.ds(h * half, half)
        u = t - begins[turn][h]
        o = u - LAG * depth

        for side in range(2):
            level = z if side == 0 else n - 1 - z
            inside = (z < owner) if side == 0 else (z > owner)
            back = z - 1 if side == 0 else z + 1
            ahead = z + 1 if side == 0 else z - 1
            c = u - LAG * level

            @pl.when(inside & (c >= 0) & (c < chunks))
            def _():
                place = chunk_rows(c)
                value = part[place, cols]

                @pl.when(level == 0)
                def _():
                    sent[turn, h, place, :] = value.astype(jnp.bfloat16)

                @pl.when(level > 0)
                def _():
                    reduce_copy(turn, h, side, c, back).wait_recv()
                    summed = value + got[turn, h, side, place, :].astype(jnp.float32)
                    sent[turn, h, place, :] = summed.astype(jnp.bfloat16)

                reduce_copy(turn, h, side, c, ahead).start()

        @pl.when((z == owner) & (o >= 0) & (o < chunks))
        def _():
            @pl.when(o == 0)
            def _():
                halo(turn, 0).wait()
                halo(turn, 1).wait()

            @pl.when(lax.rem(o, per_plane) == 0)
            def _():
                local_plane(turn, h, lax.div(o, per_plane))

            place = chunk_rows(o)
            summed = part[place, cols]
            if owner > 0:
                reduce_copy(turn, h, 0, o, z - 1).wait_recv()
                summed = summed + got[turn, h, 0, place, :].astype(jnp.float32)
            if owner < n - 1:
                reduce_copy(turn, h, 1, o, z + 1).wait_recv()
                summed = summed + got[turn, h, 1, place, :].astype(jnp.float32)
            value = (base[place, :] - scale * summed).astype(jnp.bfloat16)
            results[turn][place, cols] = value
            if owner > 0:
                result_copy(turn, h, 0, o, z - 1).start()
            if owner < n - 1:
                result_copy(turn, h, 1, o, z + 1).start()
            if turn == 0:
                ext[1, pl.ds(pl.multiple_of(rim + o * CHUNK, CHUNK), CHUNK), :] = value

                @pl.when(o == chunks - 1)
                def _():
                    halo(1, 0).start()
                    halo(1, 1).start()

        for side in range(2):
            inside = (z < owner) if side == 0 else (z > owner)
            away = owner - z if side == 0 else z - owner
            back = z + 1 if side == 0 else z - 1
            ahead = z - 1 if side == 0 else z + 1
            more = (z > 0) if side == 0 else (z < n - 1)
            b = o - LAG * away

            @pl.when(inside & (b >= 0) & (b < chunks))
            def _():
                result_copy(turn, h, side, b, back).wait_recv()

                @pl.when(more)
                def _():
                    result_copy(turn, h, side, b, ahead).start()

    def gather_half(h, t):
        ready = begins[0][h] + span
        gap = chunks // (bits + 1)
        g = 1 + h

        @pl.when(t == ready)
        def _():
            gather_start(g, first_field[:, h * half : (h + 1) * half])
            gather_send(g)

        for level in range(1, bits):
            @pl.when(t == ready + level * gap)
            def _():
                gather_forward(g, level)

        @pl.when(t == ready + chunks - 1)
        def _():
            gather_end(g)

            def keep_half(place, value):
                fields[h, place, :] = value

            pack(g, keep_half)

    def first_turn(t, carry):
        @pl.when((lax.rem(t, per_block) == 0) & (t < chunks))
        def _():
            i = lax.div(t, per_block)
            fetch(i).wait()
            place = block_rows(i)
            density = jnp.dot(orbs[place, :], points_t[...], preferred_element_type=jnp.float32)
            kbuf[place, :] = (kbuf[place, :].astype(jnp.float32) * density).astype(jnp.bfloat16)
            part[place, :] = jnp.dot(
                kbuf[place, :], points[...], preferred_element_type=jnp.float32
            )

        stream(0, 0, t)
        stream(0, 1, t)
        gather_half(0, t)
        return carry

    lax.fori_loop(0, turn_two, first_turn, 0)

    def second_turn(t, carry):
        for h in range(2):
            u = t - begins[1][h]

            @pl.when((u >= 0) & (u < chunks) & (lax.rem(t, per_block) == 0))
            def _():
                place = block_rows(lax.div(u, per_block))
                part[place, h * half : (h + 1) * half] = jnp.dot(
                    kbuf[place, :], fields[h], preferred_element_type=jnp.float32
                )

        stream(1, 0, t)
        stream(1, 1, t)
        gather_half(1, t)
        return carry

    lax.fori_loop(turn_two, turn_two + chunks + span, second_turn, 0)

    def finish(c, carry):
        for turn in range(2):
            for h, owner in enumerate(owners):
                @pl.when(z < owner)
                def _():
                    reduce_copy(turn, h, 0, c, z + 1).wait_send()

                @pl.when(z > owner)
                def _():
                    reduce_copy(turn, h, 1, c, z - 1).wait_send()

                @pl.when((z <= owner) & (z > 0))
                def _():
                    result_copy(turn, h, 0, c, z - 1).wait_send()

                @pl.when((z >= owner) & (z < n - 1))
                def _():
                    result_copy(turn, h, 1, c, z + 1).wait_send()

        return carry

    lax.fori_loop(0, chunks, finish, 0)
    for g in range(3):
        gather_sent(g)


def filtered(n, slabs, fit, orbitals, table, pot, rows, places):
    cells, total = fit.shape
    columns = orbitals.shape[1]
    half = columns // 2
    count = rows.shape[0]
    chunks = cells // CHUNK
    vmem = pl.BlockSpec(memory_space=pltpu.VMEM)
    anywhere = pl.BlockSpec(memory_space=pl.ANY)
    bf16, f32, dma = jnp.bfloat16, jnp.float32, pltpu.SemaphoreType.DMA
    return pl.pallas_call(
        functools.partial(filter_kernel, n, slabs),
        out_shape=jax.ShapeDtypeStruct((cells, columns), bf16),
        in_specs=[anywhere] * 3 + [vmem, vmem, pl.BlockSpec(memory_space=pltpu.SMEM)],
        out_specs=vmem,
        scratch_shapes=[
            pltpu.VMEM((cells, columns), bf16),
            pltpu.VMEM(table.shape, bf16),
            pltpu.VMEM((cells, total), bf16),
            pltpu.VMEM((count, cells), bf16),
            pltpu.VMEM((slabs, count + 2 * PAD, columns), bf16),
            pltpu.VMEM((slabs, count + 2 * PAD, half), bf16),
            pltpu.VMEM((slabs, count + 2 * PAD, half), bf16),
            pltpu.VMEM((total, columns), bf16),
            pltpu.VMEM((columns, total), bf16),
            pltpu.VMEM((2, total, half), bf16),
            pltpu.VMEM((cells, columns), bf16),
            pltpu.VMEM((cells, columns), f32),
            pltpu.VMEM((2, cells + 2 * WIDTH * PLANE, half), bf16),
            pltpu.VMEM((cells, half), f32),
            pltpu.VMEM((2, 2, cells, half), bf16),
            pltpu.VMEM((2, 2, 2, cells, half), bf16),
            dma((2,)),
            dma((cells // BLOCK,)),
            dma((3, 2, slabs)),
            dma((3, 2, slabs)),
            dma((2, 2, chunks)),
            dma((2, 2, 2, chunks)),
            dma((2, 2, 2, chunks)),
            dma((2, 2, chunks)),
            dma((2, 2)),
            dma((2, 2)),
        ],
        compiler_params=pltpu.CompilerParams(
            collective_id=0, has_side_effects=True, vmem_limit_bytes=VMEM_LIMIT
        ),
        cost_estimate=pl.CostEstimate(
            flops=6 * cells * total * columns, bytes_accessed=2 * cells * total, transcendentals=0
        ),
    )(fit, orbitals, table, pot, rows, places)


def rows_kernel(counts, listed, rows, places, wide):
    z = lax.axis_index("pt")
    me = lax.axis_index("slab")
    slabs = counts.shape[1]
    capacity = listed.shape[2]
    count = rows.shape[0]
    width = places.shape[0] // slabs

    def one(s, carry):
        place, mine = carry
        start = lax.div(place, ALIGN)
        slot = lax.bitwise_xor(s, me) * width
        for b in range(width):
            begin = (b + 1) * (PAD // ALIGN) - start
            places[slot + b] = jnp.clip(begin, 0, (PAD + count) // ALIGN)
        mine = jnp.where(s == me, place, mine)
        return place + counts[z, s], mine

    _, mine = lax.fori_loop(0, slabs, one, (jnp.int32(0), jnp.int32(0)))
    lane = lax.broadcasted_iota(jnp.int32, (8, capacity), 1)
    value = jnp.broadcast_to(listed[z], (8, capacity))
    wide[...] = jnp.full(wide.shape, -1.0, jnp.float32)
    wide[:, :capacity] = jnp.where(lane < counts[z, me], value, -1).astype(jnp.float32)
    moved = pltpu.roll(wide[...], lax.rem(mine, ALIGN), 1)
    rows[...] = moved.T[:count, :1].astype(jnp.int32)


def shifted_rows(owner_rows, owner_count, total):
    slabs = owner_count.shape[1]
    count = owner_rows.shape[2] + ALIGN
    lanes = (count + 127) // 128 * 128
    smem = pl.BlockSpec(memory_space=pltpu.SMEM)
    vmem = pl.BlockSpec(memory_space=pltpu.VMEM)
    return pl.pallas_call(
        rows_kernel,
        out_shape=[
            jax.ShapeDtypeStruct((count, 1), jnp.int32),
            jax.ShapeDtypeStruct((slabs * (total // PAD),), jnp.int32),
        ],
        in_specs=[smem, vmem],
        out_specs=[vmem, smem],
        scratch_shapes=[pltpu.VMEM((8, lanes), jnp.float32)],
    )(owner_count, owner_rows)


def body(n, slabs, orbitals, potential, fit_matrix, owner_rows, owner_count):
    rows, places = shifted_rows(owner_rows, owner_count, fit_matrix.shape[1])
    pot = potential.reshape(-1, PLANE)
    table = jnp.asarray(plane_table())
    return filtered(n, slabs, fit_matrix, orbitals, table, pot, rows, places)


def solution(mesh):
    placed = (P("slab", None), P("slab"), P("slab", "pt"), P(None, "slab", None), P())
    return jax.shard_map(
        functools.partial(body, mesh.shape["pt"], mesh.shape["slab"]),
        mesh=mesh, in_specs=placed, out_specs=P("slab", None), check_vma=False,
    )
```

```python
import functools

import jax
import jax.numpy as jnp
import ml_dtypes
import numpy as np
from jax import lax
from jax.experimental import pallas as pl
from jax.experimental.pallas import tpu as pltpu
from jax.sharding import PartitionSpec as P

NY = 8
NX = 32
PLANE = NY * NX
WIDTH = 4
ALIGN = 16
MESH = pl.DeviceIdType.MESH
VMEM_LIMIT = 56 * 1024 * 1024
BLOCK = 256
CHUNK = 128
LAG = 4
PAD = 128

stencil_coef = (-205.0 / 72.0, 8.0 / 5.0, -1.0 / 5.0, 8.0 / 315.0, -1.0 / 560.0)


def plane_table():
    cells = np.arange(PLANE)
    row_y, col_x = cells // NX, cells % NX
    diff_y = (row_y[:, None] - row_y[None, :]) % NY
    diff_x = (col_x[:, None] - col_x[None, :]) % NX
    same_y, same_x = diff_y == 0, diff_x == 0
    table = np.where(same_y & same_x, 3.0 * stencil_coef[0], 0.0)
    for offset in range(1, WIDTH + 1):
        for shift in (offset, -offset):
            table = table + stencil_coef[offset] * (same_y & (diff_x == shift % NX))
            table = table + stencil_coef[offset] * (same_x & (diff_y == shift % NY))
    terms, rest = [], table.astype(np.float32)
    for _ in range(3):
        term = rest.astype(ml_dtypes.bfloat16)
        terms.append(term)
        rest = rest - term.astype(np.float32)
    return np.concatenate(terms, axis=0)


def flipped(index, bit):
    size = 1 << bit
    return index + size - 2 * size * lax.rem(lax.div(index, size), 2)


def filter_kernel(
    n, slabs, fit, orbitals, table_in, pot, rows, places, out,
    orbs, table, kbuf, chosen, all_points, points_a, points_b, points, points_t, fields, first_field,
    part, ext, base, sent, got,
    insem, ksem, ag_send, ag_recv, red_send, red_recv, bc_send, bc_recv, halo_send, halo_recv,
):
    z = lax.axis_index("pt")
    s = lax.axis_index("slab")
    cells, columns = orbs.shape
    half = columns // 2
    total = kbuf.shape[1]
    count = rows.shape[0]
    bits = slabs.bit_length() - 1
    chunks = cells // CHUNK
    blocks = cells // BLOCK
    per_block = BLOCK // CHUNK
    per_plane = PLANE // CHUNK
    rim = WIDTH * PLANE
    owners = (n // 2 - 1, n // 2)
    depth = n // 2
    is_owner = (z == owners[0]) | (z == owners[1])
    upper = lax.rem(s + 1, slabs)
    lower = lax.rem(s + slabs - 1, slabs)
    results = (first_field, out)
    span = chunks + 2 * LAG * depth
    turn_two = chunks + span
    begins = ((0, chunks), (turn_two, turn_two + chunks))

    inward = [
        pltpu.make_async_copy(orbitals, orbs, insem.at[0]),
        pltpu.make_async_copy(table_in, table, insem.at[1]),
    ]
    for one in inward:
        one.start()

    def block_rows(i):
        return pl.ds(pl.multiple_of(i * BLOCK, BLOCK), BLOCK)

    def chunk_rows(c):
        return pl.ds(pl.multiple_of(c * CHUNK, CHUNK), CHUNK)

    def fetch(i):
        return pltpu.make_async_copy(
            fit.at[block_rows(i), :], kbuf.at[block_rows(i), :], ksem.at[i]
        )

    def fetch_start(i, carry):
        fetch(i).start()
        return carry

    lax.fori_loop(0, blocks, fetch_start, 0)

    barrier = pltpu.get_barrier_semaphore()
    for bit in range(bits):
        pl.semaphore_signal(
            barrier, inc=1, device_id={"slab": flipped(s, bit)}, device_id_type=MESH
        )

    @pl.when(z > 0)
    def _():
        pl.semaphore_signal(barrier, inc=1, device_id={"pt": z - 1}, device_id_type=MESH)

    @pl.when(z < n - 1)
    def _():
        pl.semaphore_signal(barrier, inc=1, device_id={"pt": z + 1}, device_id_type=MESH)

    @pl.when(is_owner)
    def _():
        pl.semaphore_signal(barrier, inc=1, device_id={"slab": upper}, device_id_type=MESH)
        pl.semaphore_signal(barrier, inc=1, device_id={"slab": lower}, device_id_type=MESH)

    for slot in range(slabs):
        all_points[slot, :PAD, :] = jnp.zeros((PAD, columns), jnp.bfloat16)
        all_points[slot, PAD + count :, :] = jnp.zeros((PAD, columns), jnp.bfloat16)
        for side_points in (points_a, points_b):
            side_points[slot, :PAD, :] = jnp.zeros((PAD, half), jnp.bfloat16)
            side_points[slot, PAD + count :, :] = jnp.zeros((PAD, half), jnp.bfloat16)

    cell_ids = lax.broadcasted_iota(jnp.int32, (count, cells), 1)
    chosen[...] = jnp.where(rows[...] == cell_ids, 1.0, 0.0).astype(jnp.bfloat16)
    for one in inward:
        one.wait()

    gathers = (all_points, points_a, points_b)
    cut = (count // 2 + ALIGN - 1) // ALIGN * ALIGN
    pieces = ((0, cut), (cut, count - cut))
    outer = list(range(1, bits))
    orders = (outer + [0], outer[::-1] + [0])
    tree = []
    for piece in range(2):
        for slot in range(1, slabs):
            place = max(i for i in range(bits) if slot >> orders[piece][i] & 1)
            tree.append((bin(slot).count("1"), piece, slot, place))
    tree.sort()

    def gather_copy(g, piece, target, place):
        bit = orders[piece][place]
        begin, size = pieces[piece]
        view = gathers[g]
        return pltpu.make_async_remote_copy(
            src_ref=view.at[target ^ (1 << bit), pl.ds(PAD + begin, size), :],
            dst_ref=view.at[target, pl.ds(PAD + begin, size), :],
            send_sem=ag_send.at[g, piece, target],
            recv_sem=ag_recv.at[g, piece, target],
            device_id={"slab": flipped(s, bit)},
            device_id_type=MESH,
        )

    def gather_start(g, field):
        picked = jnp.dot(chosen[...], field, preferred_element_type=jnp.float32)
        gathers[g][0, PAD : PAD + count, :] = picked.astype(jnp.bfloat16)

    def gather_send(g):
        for place in range(bits):
            for piece in range(2):
                gather_copy(g, piece, 1 << orders[piece][place], place).start()

    def gather_forward(g, level):
        for hops, piece, slot, place in tree:
            if hops == level and place < bits - 1:
                gather_copy(g, piece, slot, place).wait_recv()
                for later in range(place + 1, bits):
                    gather_copy(g, piece, slot | (1 << orders[piece][later]), later).start()

    def gather_end(g):
        for _, piece, slot, place in tree:
            if place == bits - 1:
                gather_copy(g, piece, slot, place).wait_recv()

    def gather_sent(g):
        for _, piece, slot, place in tree:
            gather_copy(g, piece, slot, place).wait_send()

    def pack(g, keep):
        width = total // PAD

        def one(b, carry):
            value = None
            for slot in range(slabs):
                begin = places[slot * width + b] * ALIGN
                run = gathers[g][slot, pl.ds(begin, PAD), :]
                value = run if value is None else value + run
            keep(pl.ds(pl.multiple_of(b * PAD, PAD), PAD), value)
            return carry

        lax.fori_loop(0, width, one, 0)

    gather_start(0, orbs[...])
    greeted = jnp.where(is_owner, 2, 0) + jnp.where(z > 0, 1, 0) + jnp.where(z < n - 1, 1, 0)
    pl.semaphore_wait(barrier, greeted + bits)
    gather_send(0)

    def halo(turn, k):
        src, dst, to = ((cells, 0, upper), (rim, rim + cells, lower))[k]
        return pltpu.make_async_remote_copy(
            src_ref=ext.at[turn, pl.ds(src, rim), :],
            dst_ref=ext.at[turn, pl.ds(dst, rim), :],
            send_sem=halo_send.at[turn, k],
            recv_sem=halo_recv.at[turn, k],
            device_id={"slab": to},
            device_id_type=MESH,
        )

    for h, owner in enumerate(owners):
        @pl.when(z == owner)
        def _():
            ext[0, rim : rim + cells, :] = orbs[:, h * half : (h + 1) * half]

    for level in range(1, bits):
        gather_forward(0, level)

    @pl.when(is_owner)
    def _():
        halo(0, 0).start()
        halo(0, 1).start()

    gather_end(0)

    def keep_all(place, value):
        points[place, :] = value
        points_t[:, place] = value.T

    pack(0, keep_all)

    def reduce_copy(turn, h, side, c, to):
        return pltpu.make_async_remote_copy(
            src_ref=sent.at[turn, h, chunk_rows(c), :],
            dst_ref=got.at[turn, h, side, chunk_rows(c), :],
            send_sem=red_send.at[turn, h, c],
            recv_sem=red_recv.at[turn, h, side, c],
            device_id={"pt": to},
            device_id_type=MESH,
        )

    def result_copy(turn, h, side, c, to):
        view = results[turn].at[h, chunk_rows(c), :]
        return pltpu.make_async_remote_copy(
            src_ref=view,
            dst_ref=view,
            send_sem=bc_send.at[turn, h, side, c],
            recv_sem=bc_recv.at[turn, h, c],
            device_id={"pt": to},
            device_id_type=MESH,
        )

    def local_plane(turn, h, k):
        def plane(i):
            return ext[turn, pl.ds(pl.multiple_of((k + WIDTH + i) * PLANE, PLANE), PLANE), :]

        place = pl.ds(pl.multiple_of(k * PLANE, PLANE), PLANE)
        scale = 0.5 if turn else 0.25
        centre = plane(0)
        terms = jnp.dot(table[...], centre, preferred_element_type=jnp.float32)
        summed = terms[:PLANE] + (terms[PLANE : 2 * PLANE] + terms[2 * PLANE :])
        for offset in range(1, WIDTH + 1):
            pair = plane(offset).astype(jnp.float32) + plane(-offset).astype(jnp.float32)
            summed = summed + stencil_coef[offset] * pair
        level = jnp.broadcast_to(pot[pl.ds(k, 1), :], (8, PLANE)).T[:, :1]
        value = scale * (-0.5 * summed + (level - 3.5) * centre.astype(jnp.float32))
        if turn:
            value = value - orbs[place, h * half : (h + 1) * half].astype(jnp.float32)
        base[place, :] = value

    def stream(turn, h, t):
        owner = owners[h]
        scale = 0.5 if turn else 0.25
        cols = pl.ds(h * half, half)
        u = t - begins[turn][h]
        o = u - LAG * depth

        for side in range(2):
            level = z if side == 0 else n - 1 - z
            inside = (z < owner) if side == 0 else (z > owner)
            back = z - 1 if side == 0 else z + 1
            ahead = z + 1 if side == 0 else z - 1
            c = u - LAG * level

            @pl.when(inside & (c >= 0) & (c < chunks))
            def _():
                place = chunk_rows(c)
                value = part[place, cols]

                @pl.when(level == 0)
                def _():
                    sent[turn, h, place, :] = value.astype(jnp.bfloat16)

                @pl.when(level > 0)
                def _():
                    reduce_copy(turn, h, side, c, back).wait_recv()
                    summed = value + got[turn, h, side, place, :].astype(jnp.float32)
                    sent[turn, h, place, :] = summed.astype(jnp.bfloat16)

                reduce_copy(turn, h, side, c, ahead).start()

        @pl.when((z == owner) & (o >= 0) & (o < chunks))
        def _():
            @pl.when(o == 0)
            def _():
                halo(turn, 0).wait()
                halo(turn, 1).wait()

            @pl.when(lax.rem(o, per_plane) == 0)
            def _():
                local_plane(turn, h, lax.div(o, per_plane))

            place = chunk_rows(o)
            summed = part[place, cols]
            if owner > 0:
                reduce_copy(turn, h, 0, o, z - 1).wait_recv()
                summed = summed + got[turn, h, 0, place, :].astype(jnp.float32)
            if owner < n - 1:
                reduce_copy(turn, h, 1, o, z + 1).wait_recv()
                summed = summed + got[turn, h, 1, place, :].astype(jnp.float32)
            value = (base[place, :] - scale * summed).astype(jnp.bfloat16)
            results[turn][h, place, :] = value
            if owner > 0:
                result_copy(turn, h, 0, o, z - 1).start()
            if owner < n - 1:
                result_copy(turn, h, 1, o, z + 1).start()
            if turn == 0:
                ext[1, pl.ds(pl.multiple_of(rim + o * CHUNK, CHUNK), CHUNK), :] = value

                @pl.when(o == chunks - 1)
                def _():
                    halo(1, 0).start()
                    halo(1, 1).start()

        for side in range(2):
            inside = (z < owner) if side == 0 else (z > owner)
            away = owner - z if side == 0 else z - owner
            back = z + 1 if side == 0 else z - 1
            ahead = z - 1 if side == 0 else z + 1
            more = (z > 0) if side == 0 else (z < n - 1)
            b = o - LAG * away

            @pl.when(inside & (b >= 0) & (b < chunks))
            def _():
                result_copy(turn, h, side, b, back).wait_recv()

                @pl.when(more)
                def _():
                    result_copy(turn, h, side, b, ahead).start()

    def gather_half(h, t):
        ready = begins[0][h] + span
        gap = chunks // (bits + 1)
        g = 1 + h

        @pl.when(t == ready)
        def _():
            gather_start(g, first_field[h])
            gather_send(g)

        for level in range(1, bits):
            @pl.when(t == ready + level * gap)
            def _():
                gather_forward(g, level)

        @pl.when(t == ready + chunks - 1)
        def _():
            gather_end(g)

            def keep_half(place, value):
                fields[h, place, :] = value

            pack(g, keep_half)

    def first_turn(t, carry):
        @pl.when((lax.rem(t, per_block) == 0) & (t < chunks))
        def _():
            i = lax.div(t, per_block)
            fetch(i).wait()
            place = block_rows(i)
            density = jnp.dot(orbs[place, :], points_t[...], preferred_element_type=jnp.float32)
            kbuf[place, :] = (kbuf[place, :].astype(jnp.float32) * density).astype(jnp.bfloat16)
            part[place, :] = jnp.dot(
                kbuf[place, :], points[...], preferred_element_type=jnp.float32
            )

        stream(0, 0, t)
        stream(0, 1, t)
        gather_half(0, t)
        return carry

    lax.fori_loop(0, turn_two, first_turn, 0)

    def second_turn(t, carry):
        for h in range(2):
            u = t - begins[1][h]

            @pl.when((u >= 0) & (u < chunks) & (lax.rem(t, per_block) == 0))
            def _():
                place = block_rows(lax.div(u, per_block))
                part[place, h * half : (h + 1) * half] = jnp.dot(
                    kbuf[place, :], fields[h], preferred_element_type=jnp.float32
                )

        stream(1, 0, t)
        stream(1, 1, t)
        gather_half(1, t)
        return carry

    lax.fori_loop(turn_two, turn_two + chunks + span, second_turn, 0)

    def finish(c, carry):
        for turn in range(2):
            for h, owner in enumerate(owners):
                @pl.when(z < owner)
                def _():
                    reduce_copy(turn, h, 0, c, z + 1).wait_send()

                @pl.when(z > owner)
                def _():
                    reduce_copy(turn, h, 1, c, z - 1).wait_send()

                @pl.when((z <= owner) & (z > 0))
                def _():
                    result_copy(turn, h, 0, c, z - 1).wait_send()

                @pl.when((z >= owner) & (z < n - 1))
                def _():
                    result_copy(turn, h, 1, c, z + 1).wait_send()

        return carry

    lax.fori_loop(0, chunks, finish, 0)
    for g in range(3):
        gather_sent(g)


def filtered(n, slabs, fit, orbitals, table, pot, rows, places):
    cells, total = fit.shape
    columns = orbitals.shape[1]
    half = columns // 2
    count = rows.shape[0]
    chunks = cells // CHUNK
    vmem = pl.BlockSpec(memory_space=pltpu.VMEM)
    anywhere = pl.BlockSpec(memory_space=pl.ANY)
    bf16, f32, dma = jnp.bfloat16, jnp.float32, pltpu.SemaphoreType.DMA
    return pl.pallas_call(
        functools.partial(filter_kernel, n, slabs),
        out_shape=jax.ShapeDtypeStruct((2, cells, half), bf16),
        in_specs=[anywhere] * 3 + [vmem, vmem, pl.BlockSpec(memory_space=pltpu.SMEM)],
        out_specs=vmem,
        scratch_shapes=[
            pltpu.VMEM((cells, columns), bf16),
            pltpu.VMEM(table.shape, bf16),
            pltpu.VMEM((cells, total), bf16),
            pltpu.VMEM((count, cells), bf16),
            pltpu.VMEM((slabs, count + 2 * PAD, columns), bf16),
            pltpu.VMEM((slabs, count + 2 * PAD, half), bf16),
            pltpu.VMEM((slabs, count + 2 * PAD, half), bf16),
            pltpu.VMEM((total, columns), bf16),
            pltpu.VMEM((columns, total), bf16),
            pltpu.VMEM((2, total, half), bf16),
            pltpu.VMEM((2, cells, half), bf16),
            pltpu.VMEM((cells, columns), f32),
            pltpu.VMEM((2, cells + 2 * WIDTH * PLANE, half), bf16),
            pltpu.VMEM((cells, half), f32),
            pltpu.VMEM((2, 2, cells, half), bf16),
            pltpu.VMEM((2, 2, 2, cells, half), bf16),
            dma((2,)),
            dma((cells // BLOCK,)),
            dma((3, 2, slabs)),
            dma((3, 2, slabs)),
            dma((2, 2, chunks)),
            dma((2, 2, 2, chunks)),
            dma((2, 2, 2, chunks)),
            dma((2, 2, chunks)),
            dma((2, 2)),
            dma((2, 2)),
        ],
        compiler_params=pltpu.CompilerParams(
            collective_id=0, has_side_effects=True, vmem_limit_bytes=VMEM_LIMIT
        ),
        cost_estimate=pl.CostEstimate(
            flops=6 * cells * total * columns, bytes_accessed=2 * cells * total, transcendentals=0
        ),
    )(fit, orbitals, table, pot, rows, places)


def rows_kernel(counts, listed, rows, places, wide):
    z = lax.axis_index("pt")
    me = lax.axis_index("slab")
    slabs = counts.shape[1]
    capacity = listed.shape[2]
    count = rows.shape[0]
    width = places.shape[0] // slabs

    def one(s, carry):
        place, mine = carry
        start = lax.div(place, ALIGN)
        slot = lax.bitwise_xor(s, me) * width
        for b in range(width):
            begin = (b + 1) * (PAD // ALIGN) - start
            places[slot + b] = jnp.clip(begin, 0, (PAD + count) // ALIGN)
        mine = jnp.where(s == me, place, mine)
        return place + counts[z, s], mine

    _, mine = lax.fori_loop(0, slabs, one, (jnp.int32(0), jnp.int32(0)))
    lane = lax.broadcasted_iota(jnp.int32, (8, capacity), 1)
    value = jnp.broadcast_to(listed[z], (8, capacity))
    wide[...] = jnp.full(wide.shape, -1.0, jnp.float32)
    wide[:, :capacity] = jnp.where(lane < counts[z, me], value, -1).astype(jnp.float32)
    moved = pltpu.roll(wide[...], lax.rem(mine, ALIGN), 1)
    rows[...] = moved.T[:count, :1].astype(jnp.int32)


def shifted_rows(owner_rows, owner_count, total):
    slabs = owner_count.shape[1]
    count = owner_rows.shape[2] + ALIGN
    lanes = (count + 127) // 128 * 128
    smem = pl.BlockSpec(memory_space=pltpu.SMEM)
    vmem = pl.BlockSpec(memory_space=pltpu.VMEM)
    return pl.pallas_call(
        rows_kernel,
        out_shape=[
            jax.ShapeDtypeStruct((count, 1), jnp.int32),
            jax.ShapeDtypeStruct((slabs * (total // PAD),), jnp.int32),
        ],
        in_specs=[smem, vmem],
        out_specs=[vmem, smem],
        scratch_shapes=[pltpu.VMEM((8, lanes), jnp.float32)],
    )(owner_count, owner_rows)


def body(n, slabs, orbitals, potential, fit_matrix, owner_rows, owner_count):
    rows, places = shifted_rows(owner_rows, owner_count, fit_matrix.shape[1])
    pot = potential.reshape(-1, PLANE)
    table = jnp.asarray(plane_table())
    halves = filtered(n, slabs, fit_matrix, orbitals, table, pot, rows, places)
    return jnp.concatenate([halves[0], halves[1]], axis=1)


def solution(mesh):
    placed = (P("slab", None), P("slab"), P("slab", "pt"), P(None, "slab", None), P())
    return jax.shard_map(
        functools.partial(body, mesh.shape["pt"], mesh.shape["slab"]),
        mesh=mesh, in_specs=placed, out_specs=P("slab", None), check_vma=False,
    )
```

```python
import functools

import jax
import jax.numpy as jnp
import ml_dtypes
import numpy as np
from jax import lax
from jax.experimental import pallas as pl
from jax.experimental.pallas import tpu as pltpu
from jax.sharding import PartitionSpec as P

NY = 8
NX = 32
PLANE = NY * NX
WIDTH = 4
ALIGN = 16
MESH = pl.DeviceIdType.MESH
VMEM_LIMIT = 56 * 1024 * 1024
BLOCK = 256
CHUNK = 128
LAG = 3
PAD = 128

stencil_coef = (-205.0 / 72.0, 8.0 / 5.0, -1.0 / 5.0, 8.0 / 315.0, -1.0 / 560.0)


def plane_table():
    cells = np.arange(PLANE)
    row_y, col_x = cells // NX, cells % NX
    diff_y = (row_y[:, None] - row_y[None, :]) % NY
    diff_x = (col_x[:, None] - col_x[None, :]) % NX
    same_y, same_x = diff_y == 0, diff_x == 0
    table = np.where(same_y & same_x, 3.0 * stencil_coef[0], 0.0)
    for offset in range(1, WIDTH + 1):
        for shift in (offset, -offset):
            table = table + stencil_coef[offset] * (same_y & (diff_x == shift % NX))
            table = table + stencil_coef[offset] * (same_x & (diff_y == shift % NY))
    terms, rest = [], table.astype(np.float32)
    for _ in range(3):
        term = rest.astype(ml_dtypes.bfloat16)
        terms.append(term)
        rest = rest - term.astype(np.float32)
    return np.concatenate(terms, axis=0)


def flipped(index, bit):
    size = 1 << bit
    return index + size - 2 * size * lax.rem(lax.div(index, size), 2)


def filter_kernel(
    n, slabs, fit, orbitals, table_in, pot, rows, places, out,
    orbs, table, kbuf, chosen, all_points, points_a, points_b, points, points_t, fields, first_field,
    part, ext, base, sent, got,
    insem, ksem, ag_send, ag_recv, red_send, red_recv, bc_send, bc_recv, halo_send, halo_recv,
):
    z = lax.axis_index("pt")
    s = lax.axis_index("slab")
    cells, columns = orbs.shape
    half = columns // 2
    total = kbuf.shape[1]
    count = rows.shape[0]
    bits = slabs.bit_length() - 1
    chunks = cells // CHUNK
    blocks = cells // BLOCK
    per_block = BLOCK // CHUNK
    per_plane = PLANE // CHUNK
    rim = WIDTH * PLANE
    owners = (n // 2 - 1, n // 2)
    depth = n // 2
    is_owner = (z == owners[0]) | (z == owners[1])
    upper = lax.rem(s + 1, slabs)
    lower = lax.rem(s + slabs - 1, slabs)
    results = (first_field, out)
    span = chunks + 2 * LAG * depth
    turn_two = chunks + span
    begins = ((0, chunks), (turn_two, turn_two + chunks))

    inward = [
        pltpu.make_async_copy(orbitals, orbs, insem.at[0]),
        pltpu.make_async_copy(table_in, table, insem.at[1]),
    ]
    for one in inward:
        one.start()

    def block_rows(i):
        return pl.ds(pl.multiple_of(i * BLOCK, BLOCK), BLOCK)

    def chunk_rows(c):
        return pl.ds(pl.multiple_of(c * CHUNK, CHUNK), CHUNK)

    def fetch(i):
        return pltpu.make_async_copy(
            fit.at[block_rows(i), :], kbuf.at[block_rows(i), :], ksem.at[i]
        )

    def fetch_start(i, carry):
        fetch(i).start()
        return carry

    lax.fori_loop(0, blocks, fetch_start, 0)

    barrier = pltpu.get_barrier_semaphore()
    for bit in range(bits):
        pl.semaphore_signal(
            barrier, inc=1, device_id={"slab": flipped(s, bit)}, device_id_type=MESH
        )

    @pl.when(z > 0)
    def _():
        pl.semaphore_signal(barrier, inc=1, device_id={"pt": z - 1}, device_id_type=MESH)

    @pl.when(z < n - 1)
    def _():
        pl.semaphore_signal(barrier, inc=1, device_id={"pt": z + 1}, device_id_type=MESH)

    @pl.when(is_owner)
    def _():
        pl.semaphore_signal(barrier, inc=1, device_id={"slab": upper}, device_id_type=MESH)
        pl.semaphore_signal(barrier, inc=1, device_id={"slab": lower}, device_id_type=MESH)

    for slot in range(slabs):
        all_points[slot, :PAD, :] = jnp.zeros((PAD, columns), jnp.bfloat16)
        all_points[slot, PAD + count :, :] = jnp.zeros((PAD, columns), jnp.bfloat16)
        for side_points in (points_a, points_b):
            side_points[slot, :PAD, :] = jnp.zeros((PAD, half), jnp.bfloat16)
            side_points[slot, PAD + count :, :] = jnp.zeros((PAD, half), jnp.bfloat16)

    cell_ids = lax.broadcasted_iota(jnp.int32, (count, cells), 1)
    chosen[...] = jnp.where(rows[...] == cell_ids, 1.0, 0.0).astype(jnp.bfloat16)
    for one in inward:
        one.wait()

    gathers = (all_points, points_a, points_b)
    cut = (count // 2 + ALIGN - 1) // ALIGN * ALIGN
    pieces = ((0, cut), (cut, count - cut))
    outer = list(range(1, bits))
    orders = (outer + [0], outer[::-1] + [0])
    tree = []
    for piece in range(2):
        for slot in range(1, slabs):
            place = max(i for i in range(bits) if slot >> orders[piece][i] & 1)
            tree.append((bin(slot).count("1"), piece, slot, place))
    tree.sort()

    def gather_copy(g, piece, target, place):
        bit = orders[piece][place]
        begin, size = pieces[piece]
        view = gathers[g]
        return pltpu.make_async_remote_copy(
            src_ref=view.at[target ^ (1 << bit), pl.ds(PAD + begin, size), :],
            dst_ref=view.at[target, pl.ds(PAD + begin, size), :],
            send_sem=ag_send.at[g, piece, target],
            recv_sem=ag_recv.at[g, piece, target],
            device_id={"slab": flipped(s, bit)},
            device_id_type=MESH,
        )

    def gather_start(g, field):
        picked = jnp.dot(chosen[...], field, preferred_element_type=jnp.float32)
        gathers[g][0, PAD : PAD + count, :] = picked.astype(jnp.bfloat16)

    def gather_send(g):
        for place in range(bits):
            for piece in range(2):
                gather_copy(g, piece, 1 << orders[piece][place], place).start()

    def gather_forward(g, level):
        for hops, piece, slot, place in tree:
            if hops == level and place < bits - 1:
                gather_copy(g, piece, slot, place).wait_recv()
                for later in range(place + 1, bits):
                    gather_copy(g, piece, slot | (1 << orders[piece][later]), later).start()

    def gather_end(g):
        for _, piece, slot, place in tree:
            if place == bits - 1:
                gather_copy(g, piece, slot, place).wait_recv()

    def gather_sent(g):
        for _, piece, slot, place in tree:
            gather_copy(g, piece, slot, place).wait_send()

    def pack(g, keep):
        width = total // PAD

        def one(b, carry):
            value = None
            for slot in range(slabs):
                begin = places[slot * width + b] * ALIGN
                run = gathers[g][slot, pl.ds(begin, PAD), :]
                value = run if value is None else value + run
            keep(pl.ds(pl.multiple_of(b * PAD, PAD), PAD), value)
            return carry

        lax.fori_loop(0, width, one, 0)

    gather_start(0, orbs[...])
    greeted = jnp.where(is_owner, 2, 0) + jnp.where(z > 0, 1, 0) + jnp.where(z < n - 1, 1, 0)
    pl.semaphore_wait(barrier, greeted + bits)
    gather_send(0)

    def halo(turn, k):
        src, dst, to = ((cells, 0, upper), (rim, rim + cells, lower))[k]
        return pltpu.make_async_remote_copy(
            src_ref=ext.at[turn, pl.ds(src, rim), :],
            dst_ref=ext.at[turn, pl.ds(dst, rim), :],
            send_sem=halo_send.at[turn, k],
            recv_sem=halo_recv.at[turn, k],
            device_id={"slab": to},
            device_id_type=MESH,
        )

    for h, owner in enumerate(owners):
        @pl.when(z == owner)
        def _():
            ext[0, rim : rim + cells, :] = orbs[:, h * half : (h + 1) * half]

    for level in range(1, bits):
        gather_forward(0, level)

    @pl.when(is_owner)
    def _():
        halo(0, 0).start()
        halo(0, 1).start()

    gather_end(0)

    def keep_all(place, value):
        points[place, :] = value
        points_t[:, place] = value.T

    pack(0, keep_all)

    def reduce_copy(turn, h, side, c, to):
        return pltpu.make_async_remote_copy(
            src_ref=sent.at[turn, h, chunk_rows(c), :],
            dst_ref=got.at[turn, h, side, chunk_rows(c), :],
            send_sem=red_send.at[turn, h, c],
            recv_sem=red_recv.at[turn, h, side, c],
            device_id={"pt": to},
            device_id_type=MESH,
        )

    def result_copy(turn, h, side, c, to):
        view = results[turn].at[h, chunk_rows(c), :]
        return pltpu.make_async_remote_copy(
            src_ref=view,
            dst_ref=view,
            send_sem=bc_send.at[turn, h, side, c],
            recv_sem=bc_recv.at[turn, h, c],
            device_id={"pt": to},
            device_id_type=MESH,
        )

    def local_plane(turn, h, k):
        def plane(i):
            return ext[turn, pl.ds(pl.multiple_of((k + WIDTH + i) * PLANE, PLANE), PLANE), :]

        place = pl.ds(pl.multiple_of(k * PLANE, PLANE), PLANE)
        scale = 0.5 if turn else 0.25
        centre = plane(0)
        terms = jnp.dot(table[...], centre, preferred_element_type=jnp.float32)
        summed = terms[:PLANE] + (terms[PLANE : 2 * PLANE] + terms[2 * PLANE :])
        for offset in range(1, WIDTH + 1):
            pair = plane(offset).astype(jnp.float32) + plane(-offset).astype(jnp.float32)
            summed = summed + stencil_coef[offset] * pair
        level = jnp.broadcast_to(pot[pl.ds(k, 1), :], (8, PLANE)).T[:, :1]
        value = scale * (-0.5 * summed + (level - 3.5) * centre.astype(jnp.float32))
        if turn:
            value = value - orbs[place, h * half : (h + 1) * half].astype(jnp.float32)
        base[place, :] = value

    def stream(turn, h, t):
        owner = owners[h]
        scale = 0.5 if turn else 0.25
        cols = pl.ds(h * half, half)
        u = t - begins[turn][h]
        o = u - LAG * depth

        for side in range(2):
            level = z if side == 0 else n - 1 - z
            inside = (z < owner) if side == 0 else (z > owner)
            back = z - 1 if side == 0 else z + 1
            ahead = z + 1 if side == 0 else z - 1
            c = u - LAG * level

            @pl.when(inside & (c >= 0) & (c < chunks))
            def _():
                place = chunk_rows(c)
                value = part[place, cols]

                @pl.when(level == 0)
                def _():
                    sent[turn, h, place, :] = value.astype(jnp.bfloat16)

                @pl.when(level > 0)
                def _():
                    reduce_copy(turn, h, side, c, back).wait_recv()
                    summed = value + got[turn, h, side, place, :].astype(jnp.float32)
                    sent[turn, h, place, :] = summed.astype(jnp.bfloat16)

                reduce_copy(turn, h, side, c, ahead).start()

        @pl.when((z == owner) & (o >= 0) & (o < chunks))
        def _():
            @pl.when(o == 0)
            def _():
                halo(turn, 0).wait()
                halo(turn, 1).wait()

            @pl.when(lax.rem(o, per_plane) == 0)
            def _():
                local_plane(turn, h, lax.div(o, per_plane))

            place = chunk_rows(o)
            summed = part[place, cols]
            if owner > 0:
                reduce_copy(turn, h, 0, o, z - 1).wait_recv()
                summed = summed + got[turn, h, 0, place, :].astype(jnp.float32)
            if owner < n - 1:
                reduce_copy(turn, h, 1, o, z + 1).wait_recv()
                summed = summed + got[turn, h, 1, place, :].astype(jnp.float32)
            value = (base[place, :] - scale * summed).astype(jnp.bfloat16)
            results[turn][h, place, :] = value
            if owner > 0:
                result_copy(turn, h, 0, o, z - 1).start()
            if owner < n - 1:
                result_copy(turn, h, 1, o, z + 1).start()
            if turn == 0:
                ext[1, pl.ds(pl.multiple_of(rim + o * CHUNK, CHUNK), CHUNK), :] = value

                @pl.when(o == chunks - 1)
                def _():
                    halo(1, 0).start()
                    halo(1, 1).start()

        for side in range(2):
            inside = (z < owner) if side == 0 else (z > owner)
            away = owner - z if side == 0 else z - owner
            back = z + 1 if side == 0 else z - 1
            ahead = z - 1 if side == 0 else z + 1
            more = (z > 0) if side == 0 else (z < n - 1)
            b = o - LAG * away

            @pl.when(inside & (b >= 0) & (b < chunks))
            def _():
                result_copy(turn, h, side, b, back).wait_recv()

                @pl.when(more)
                def _():
                    result_copy(turn, h, side, b, ahead).start()

    def gather_half(h, t):
        ready = begins[0][h] + span
        gap = chunks // (bits + 1)
        g = 1 + h

        @pl.when(t == ready)
        def _():
            gather_start(g, first_field[h])
            gather_send(g)

        for level in range(1, bits):
            @pl.when(t == ready + level * gap)
            def _():
                gather_forward(g, level)

        @pl.when(t == ready + chunks - 1)
        def _():
            gather_end(g)

            def keep_half(place, value):
                fields[h, place, :] = value

            pack(g, keep_half)

    def first_turn(t, carry):
        @pl.when((lax.rem(t, per_block) == 0) & (t < chunks))
        def _():
            i = lax.div(t, per_block)
            fetch(i).wait()
            place = block_rows(i)
            density = jnp.dot(orbs[place, :], points_t[...], preferred_element_type=jnp.float32)
            kbuf[place, :] = (kbuf[place, :].astype(jnp.float32) * density).astype(jnp.bfloat16)
            part[place, :] = jnp.dot(
                kbuf[place, :], points[...], preferred_element_type=jnp.float32
            )

        stream(0, 0, t)
        stream(0, 1, t)
        gather_half(0, t)
        return carry

    lax.fori_loop(0, turn_two, first_turn, 0)

    def second_turn(t, carry):
        for h in range(2):
            u = t - begins[1][h]

            @pl.when((u >= 0) & (u < chunks) & (lax.rem(t, per_block) == 0))
            def _():
                place = block_rows(lax.div(u, per_block))
                part[place, h * half : (h + 1) * half] = jnp.dot(
                    kbuf[place, :], fields[h], preferred_element_type=jnp.float32
                )

        stream(1, 0, t)
        stream(1, 1, t)
        gather_half(1, t)
        return carry

    lax.fori_loop(turn_two, turn_two + chunks + span, second_turn, 0)

    def finish(c, carry):
        for turn in range(2):
            for h, owner in enumerate(owners):
                @pl.when(z < owner)
                def _():
                    reduce_copy(turn, h, 0, c, z + 1).wait_send()

                @pl.when(z > owner)
                def _():
                    reduce_copy(turn, h, 1, c, z - 1).wait_send()

                @pl.when((z <= owner) & (z > 0))
                def _():
                    result_copy(turn, h, 0, c, z - 1).wait_send()

                @pl.when((z >= owner) & (z < n - 1))
                def _():
                    result_copy(turn, h, 1, c, z + 1).wait_send()

        return carry

    lax.fori_loop(0, chunks, finish, 0)
    for g in range(3):
        gather_sent(g)


def filtered(n, slabs, fit, orbitals, table, pot, rows, places):
    cells, total = fit.shape
    columns = orbitals.shape[1]
    half = columns // 2
    count = rows.shape[0]
    chunks = cells // CHUNK
    vmem = pl.BlockSpec(memory_space=pltpu.VMEM)
    anywhere = pl.BlockSpec(memory_space=pl.ANY)
    bf16, f32, dma = jnp.bfloat16, jnp.float32, pltpu.SemaphoreType.DMA
    return pl.pallas_call(
        functools.partial(filter_kernel, n, slabs),
        out_shape=jax.ShapeDtypeStruct((2, cells, half), bf16),
        in_specs=[anywhere] * 3 + [vmem, vmem, pl.BlockSpec(memory_space=pltpu.SMEM)],
        out_specs=vmem,
        scratch_shapes=[
            pltpu.VMEM((cells, columns), bf16),
            pltpu.VMEM(table.shape, bf16),
            pltpu.VMEM((cells, total), bf16),
            pltpu.VMEM((count, cells), bf16),
            pltpu.VMEM((slabs, count + 2 * PAD, columns), bf16),
            pltpu.VMEM((slabs, count + 2 * PAD, half), bf16),
            pltpu.VMEM((slabs, count + 2 * PAD, half), bf16),
            pltpu.VMEM((total, columns), bf16),
            pltpu.VMEM((columns, total), bf16),
            pltpu.VMEM((2, total, half), bf16),
            pltpu.VMEM((2, cells, half), bf16),
            pltpu.VMEM((cells, columns), f32),
            pltpu.VMEM((2, cells + 2 * WIDTH * PLANE, half), bf16),
            pltpu.VMEM((cells, half), f32),
            pltpu.VMEM((2, 2, cells, half), bf16),
            pltpu.VMEM((2, 2, 2, cells, half), bf16),
            dma((2,)),
            dma((cells // BLOCK,)),
            dma((3, 2, slabs)),
            dma((3, 2, slabs)),
            dma((2, 2, chunks)),
            dma((2, 2, 2, chunks)),
            dma((2, 2, 2, chunks)),
            dma((2, 2, chunks)),
            dma((2, 2)),
            dma((2, 2)),
        ],
        compiler_params=pltpu.CompilerParams(
            collective_id=0, has_side_effects=True, vmem_limit_bytes=VMEM_LIMIT
        ),
        cost_estimate=pl.CostEstimate(
            flops=6 * cells * total * columns, bytes_accessed=2 * cells * total, transcendentals=0
        ),
    )(fit, orbitals, table, pot, rows, places)


def rows_kernel(counts, listed, rows, places, wide):
    z = lax.axis_index("pt")
    me = lax.axis_index("slab")
    slabs = counts.shape[1]
    capacity = listed.shape[2]
    count = rows.shape[0]
    width = places.shape[0] // slabs

    def one(s, carry):
        place, mine = carry
        start = lax.div(place, ALIGN)
        slot = lax.bitwise_xor(s, me) * width
        for b in range(width):
            begin = (b + 1) * (PAD // ALIGN) - start
            places[slot + b] = jnp.clip(begin, 0, (PAD + count) // ALIGN)
        mine = jnp.where(s == me, place, mine)
        return place + counts[z, s], mine

    _, mine = lax.fori_loop(0, slabs, one, (jnp.int32(0), jnp.int32(0)))
    lane = lax.broadcasted_iota(jnp.int32, (8, capacity), 1)
    value = jnp.broadcast_to(listed[z], (8, capacity))
    wide[...] = jnp.full(wide.shape, -1.0, jnp.float32)
    wide[:, :capacity] = jnp.where(lane < counts[z, me], value, -1).astype(jnp.float32)
    moved = pltpu.roll(wide[...], lax.rem(mine, ALIGN), 1)
    rows[...] = moved.T[:count, :1].astype(jnp.int32)


def shifted_rows(owner_rows, owner_count, total):
    slabs = owner_count.shape[1]
    count = owner_rows.shape[2] + ALIGN
    lanes = (count + 127) // 128 * 128
    smem = pl.BlockSpec(memory_space=pltpu.SMEM)
    vmem = pl.BlockSpec(memory_space=pltpu.VMEM)
    return pl.pallas_call(
        rows_kernel,
        out_shape=[
            jax.ShapeDtypeStruct((count, 1), jnp.int32),
            jax.ShapeDtypeStruct((slabs * (total // PAD),), jnp.int32),
        ],
        in_specs=[smem, vmem],
        out_specs=[vmem, smem],
        scratch_shapes=[pltpu.VMEM((8, lanes), jnp.float32)],
    )(owner_count, owner_rows)


def body(n, slabs, orbitals, potential, fit_matrix, owner_rows, owner_count):
    rows, places = shifted_rows(owner_rows, owner_count, fit_matrix.shape[1])
    pot = potential.reshape(-1, PLANE)
    table = jnp.asarray(plane_table())
    halves = filtered(n, slabs, fit_matrix, orbitals, table, pot, rows, places)
    return jnp.concatenate([halves[0], halves[1]], axis=1)


def solution(mesh):
    placed = (P("slab", None), P("slab"), P("slab", "pt"), P(None, "slab", None), P())
    return jax.shard_map(
        functools.partial(body, mesh.shape["pt"], mesh.shape["slab"]),
        mesh=mesh, in_specs=placed, out_specs=P("slab", None), check_vma=False,
    )
```

```python
import functools

import jax
import jax.numpy as jnp
import ml_dtypes
import numpy as np
from jax import lax
from jax.experimental import pallas as pl
from jax.experimental.pallas import tpu as pltpu
from jax.sharding import PartitionSpec as P

NY = 8
NX = 32
PLANE = NY * NX
WIDTH = 4
ALIGN = 16
MESH = pl.DeviceIdType.MESH
VMEM_LIMIT = 56 * 1024 * 1024
BLOCK = 256
CHUNK = 128
LAG = 4
PAD = 128

stencil_coef = (-205.0 / 72.0, 8.0 / 5.0, -1.0 / 5.0, 8.0 / 315.0, -1.0 / 560.0)


def plane_table():
    cells = np.arange(PLANE)
    row_y, col_x = cells // NX, cells % NX
    diff_y = (row_y[:, None] - row_y[None, :]) % NY
    diff_x = (col_x[:, None] - col_x[None, :]) % NX
    same_y, same_x = diff_y == 0, diff_x == 0
    table = np.where(same_y & same_x, 3.0 * stencil_coef[0], 0.0)
    for offset in range(1, WIDTH + 1):
        for shift in (offset, -offset):
            table = table + stencil_coef[offset] * (same_y & (diff_x == shift % NX))
            table = table + stencil_coef[offset] * (same_x & (diff_y == shift % NY))
    terms, rest = [], table.astype(np.float32)
    for _ in range(3):
        term = rest.astype(ml_dtypes.bfloat16)
        terms.append(term)
        rest = rest - term.astype(np.float32)
    return np.concatenate(terms, axis=0)


def flipped(index, bit):
    size = 1 << bit
    return index + size - 2 * size * lax.rem(lax.div(index, size), 2)


def filter_kernel(
    n, slabs, fit, orbitals, table_in, pot, rows, places, out,
    orbs, table, kbuf, chosen, all_points, points_a, points_b, points, points_t, fields, first_field,
    part, ext, base, sent, got,
    insem, ksem, ag_send, ag_recv, red_send, red_recv, bc_send, bc_recv, halo_send, halo_recv,
):
    z = lax.axis_index("pt")
    s = lax.axis_index("slab")
    cells, columns = orbs.shape
    half = columns // 2
    total = kbuf.shape[1]
    count = rows.shape[0]
    bits = slabs.bit_length() - 1
    chunks = cells // CHUNK
    blocks = cells // BLOCK
    per_block = BLOCK // CHUNK
    per_plane = PLANE // CHUNK
    rim = WIDTH * PLANE
    owners = (n // 2 - 1, n // 2)
    depth = n // 2
    is_owner = (z == owners[0]) | (z == owners[1])
    upper = lax.rem(s + 1, slabs)
    lower = lax.rem(s + slabs - 1, slabs)
    results = (first_field, out)
    span = chunks + 2 * LAG * depth
    turn_two = chunks + span
    begins = ((0, chunks), (turn_two, turn_two + chunks))

    inward = [
        pltpu.make_async_copy(orbitals, orbs, insem.at[0]),
        pltpu.make_async_copy(table_in, table, insem.at[1]),
    ]
    for one in inward:
        one.start()

    def block_rows(i):
        return pl.ds(pl.multiple_of(i * BLOCK, BLOCK), BLOCK)

    def chunk_rows(c):
        return pl.ds(pl.multiple_of(c * CHUNK, CHUNK), CHUNK)

    def fetch(i):
        return pltpu.make_async_copy(
            fit.at[block_rows(i), :], kbuf.at[block_rows(i), :], ksem.at[i]
        )

    def fetch_start(i, carry):
        fetch(i).start()
        return carry

    lax.fori_loop(0, blocks, fetch_start, 0)

    barrier = pltpu.get_barrier_semaphore()
    for bit in range(bits):
        pl.semaphore_signal(
            barrier, inc=1, device_id={"slab": flipped(s, bit)}, device_id_type=MESH
        )

    @pl.when(z > 0)
    def _():
        pl.semaphore_signal(barrier, inc=1, device_id={"pt": z - 1}, device_id_type=MESH)

    @pl.when(z < n - 1)
    def _():
        pl.semaphore_signal(barrier, inc=1, device_id={"pt": z + 1}, device_id_type=MESH)

    @pl.when(is_owner)
    def _():
        pl.semaphore_signal(barrier, inc=1, device_id={"slab": upper}, device_id_type=MESH)
        pl.semaphore_signal(barrier, inc=1, device_id={"slab": lower}, device_id_type=MESH)

    for slot in range(slabs):
        all_points[slot, :PAD, :] = jnp.zeros((PAD, columns), jnp.bfloat16)
        all_points[slot, PAD + count :, :] = jnp.zeros((PAD, columns), jnp.bfloat16)
        for side_points in (points_a, points_b):
            side_points[slot, :PAD, :] = jnp.zeros((PAD, half), jnp.bfloat16)
            side_points[slot, PAD + count :, :] = jnp.zeros((PAD, half), jnp.bfloat16)

    cell_ids = lax.broadcasted_iota(jnp.int32, (count, cells), 1)
    chosen[...] = jnp.where(rows[...] == cell_ids, 1.0, 0.0).astype(jnp.bfloat16)
    for one in inward:
        one.wait()

    gathers = (all_points, points_a, points_b)
    cut = (count // 2 + ALIGN - 1) // ALIGN * ALIGN
    pieces = ((0, cut), (cut, count - cut))
    outer = list(range(1, bits))
    orders = (outer + [0], outer[::-1] + [0])
    tree = []
    for piece in range(2):
        for slot in range(1, slabs):
            place = max(i for i in range(bits) if slot >> orders[piece][i] & 1)
            tree.append((bin(slot).count("1"), piece, slot, place))
    tree.sort()

    def gather_copy(g, piece, target, place):
        bit = orders[piece][place]
        begin, size = pieces[piece]
        view = gathers[g]
        return pltpu.make_async_remote_copy(
            src_ref=view.at[target ^ (1 << bit), pl.ds(PAD + begin, size), :],
            dst_ref=view.at[target, pl.ds(PAD + begin, size), :],
            send_sem=ag_send.at[g, piece, target],
            recv_sem=ag_recv.at[g, piece, target],
            device_id={"slab": flipped(s, bit)},
            device_id_type=MESH,
        )

    def gather_start(g, field):
        picked = jnp.dot(chosen[...], field, preferred_element_type=jnp.float32)
        gathers[g][0, PAD : PAD + count, :] = picked.astype(jnp.bfloat16)

    def gather_send(g):
        for place in range(bits):
            for piece in range(2):
                gather_copy(g, piece, 1 << orders[piece][place], place).start()

    def gather_forward(g, level):
        for hops, piece, slot, place in tree:
            if hops == level and place < bits - 1:
                gather_copy(g, piece, slot, place).wait_recv()
                for later in range(place + 1, bits):
                    gather_copy(g, piece, slot | (1 << orders[piece][later]), later).start()

    def gather_end(g):
        for _, piece, slot, place in tree:
            if place == bits - 1:
                gather_copy(g, piece, slot, place).wait_recv()

    def gather_sent(g):
        for _, piece, slot, place in tree:
            gather_copy(g, piece, slot, place).wait_send()

    def pack(g, keep):
        width = total // PAD

        def one(b, carry):
            value = None
            for slot in range(slabs):
                begin = places[slot * width + b] * ALIGN
                run = gathers[g][slot, pl.ds(begin, PAD), :]
                value = run if value is None else value + run
            keep(pl.ds(pl.multiple_of(b * PAD, PAD), PAD), value)
            return carry

        lax.fori_loop(0, width, one, 0)

    gather_start(0, orbs[...])
    greeted = jnp.where(is_owner, 2, 0) + jnp.where(z > 0, 1, 0) + jnp.where(z < n - 1, 1, 0)
    pl.semaphore_wait(barrier, greeted + bits)
    gather_send(0)

    def halo(turn, k):
        src, dst, to = ((cells, 0, upper), (rim, rim + cells, lower))[k]
        return pltpu.make_async_remote_copy(
            src_ref=ext.at[turn, pl.ds(src, rim), :],
            dst_ref=ext.at[turn, pl.ds(dst, rim), :],
            send_sem=halo_send.at[turn, k],
            recv_sem=halo_recv.at[turn, k],
            device_id={"slab": to},
            device_id_type=MESH,
        )

    for h, owner in enumerate(owners):
        @pl.when(z == owner)
        def _():
            ext[0, rim : rim + cells, :] = orbs[:, h * half : (h + 1) * half]

    for level in range(1, bits):
        gather_forward(0, level)

    @pl.when(is_owner)
    def _():
        halo(0, 0).start()
        halo(0, 1).start()

    gather_end(0)

    def keep_all(place, value):
        points[place, :] = value
        points_t[:, place] = value.T

    pack(0, keep_all)

    def reduce_copy(turn, h, side, c, to):
        return pltpu.make_async_remote_copy(
            src_ref=sent.at[turn, h, chunk_rows(c), :],
            dst_ref=got.at[turn, h, side, chunk_rows(c), :],
            send_sem=red_send.at[turn, h, c],
            recv_sem=red_recv.at[turn, h, side, c],
            device_id={"pt": to},
            device_id_type=MESH,
        )

    def result_copy(turn, h, side, c, to):
        view = results[turn].at[h, chunk_rows(c), :]
        return pltpu.make_async_remote_copy(
            src_ref=view,
            dst_ref=view,
            send_sem=bc_send.at[turn, h, side, c],
            recv_sem=bc_recv.at[turn, h, c],
            device_id={"pt": to},
            device_id_type=MESH,
        )

    def local_plane(turn, h, k):
        def plane(i):
            return ext[turn, pl.ds(pl.multiple_of((k + WIDTH + i) * PLANE, PLANE), PLANE), :]

        place = pl.ds(pl.multiple_of(k * PLANE, PLANE), PLANE)
        scale = 0.5 if turn else 0.25
        centre = plane(0)
        terms = jnp.dot(table[...], centre, preferred_element_type=jnp.float32)
        summed = terms[:PLANE] + (terms[PLANE : 2 * PLANE] + terms[2 * PLANE :])
        for offset in range(1, WIDTH + 1):
            pair = plane(offset).astype(jnp.float32) + plane(-offset).astype(jnp.float32)
            summed = summed + stencil_coef[offset] * pair
        level = jnp.broadcast_to(pot[pl.ds(k, 1), :], (8, PLANE)).T[:, :1]
        value = scale * (-0.5 * summed + (level - 3.5) * centre.astype(jnp.float32))
        if turn:
            value = value - orbs[place, h * half : (h + 1) * half].astype(jnp.float32)
        base[place, :] = value

    def stream(turn, h, t):
        owner = owners[h]
        scale = 0.5 if turn else 0.25
        cols = pl.ds(h * half, half)
        u = t - begins[turn][h]
        o = u - LAG * depth

        for side in range(2):
            level = z if side == 0 else n - 1 - z
            inside = (z < owner) if side == 0 else (z > owner)
            back = z - 1 if side == 0 else z + 1
            ahead = z + 1 if side == 0 else z - 1
            c = u - LAG * level

            @pl.when(inside & (c >= 0) & (c < chunks))
            def _():
                place = chunk_rows(c)
                value = part[place, cols]

                @pl.when(level == 0)
                def _():
                    sent[turn, h, place, :] = value.astype(jnp.bfloat16)

                @pl.when(level > 0)
                def _():
                    reduce_copy(turn, h, side, c, back).wait_recv()
                    summed = value + got[turn, h, side, place, :].astype(jnp.float32)
                    sent[turn, h, place, :] = summed.astype(jnp.bfloat16)

                reduce_copy(turn, h, side, c, ahead).start()

        @pl.when((z == owner) & (o >= 0) & (o < chunks))
        def _():
            @pl.when(o == 0)
            def _():
                halo(turn, 0).wait()
                halo(turn, 1).wait()

            @pl.when(lax.rem(o, per_plane) == 0)
            def _():
                local_plane(turn, h, lax.div(o, per_plane))

            place = chunk_rows(o)
            summed = part[place, cols]
            if owner > 0:
                reduce_copy(turn, h, 0, o, z - 1).wait_recv()
                summed = summed + got[turn, h, 0, place, :].astype(jnp.float32)
            if owner < n - 1:
                reduce_copy(turn, h, 1, o, z + 1).wait_recv()
                summed = summed + got[turn, h, 1, place, :].astype(jnp.float32)
            value = (base[place, :] - scale * summed).astype(jnp.bfloat16)
            results[turn][h, place, :] = value
            if owner > 0:
                result_copy(turn, h, 0, o, z - 1).start()
            if owner < n - 1:
                result_copy(turn, h, 1, o, z + 1).start()
            if turn == 0:
                ext[1, pl.ds(pl.multiple_of(rim + o * CHUNK, CHUNK), CHUNK), :] = value

                @pl.when(o == chunks - 1)
                def _():
                    halo(1, 0).start()
                    halo(1, 1).start()

        for side in range(2):
            inside = (z < owner) if side == 0 else (z > owner)
            away = owner - z if side == 0 else z - owner
            back = z + 1 if side == 0 else z - 1
            ahead = z - 1 if side == 0 else z + 1
            more = (z > 0) if side == 0 else (z < n - 1)
            b = o - LAG * away

            @pl.when(inside & (b >= 0) & (b < chunks))
            def _():
                result_copy(turn, h, side, b, back).wait_recv()

                @pl.when(more)
                def _():
                    result_copy(turn, h, side, b, ahead).start()

    def gather_half(h, t):
        ready = begins[0][h] + span
        gap = chunks // (bits + 1)
        g = 1 + h

        @pl.when(t == ready)
        def _():
            gather_start(g, first_field[h])
            gather_send(g)

        for level in range(1, bits):
            @pl.when(t == ready + level * gap)
            def _():
                gather_forward(g, level)

        @pl.when(t == ready + chunks - 1)
        def _():
            gather_end(g)

            def keep_half(place, value):
                fields[h, place, :] = value

            pack(g, keep_half)

    def kernel_block(i):
        fetch(i).wait()
        place = block_rows(i)
        density = jnp.dot(orbs[place, :], points_t[...], preferred_element_type=jnp.float32)
        kbuf[place, :] = (kbuf[place, :].astype(jnp.float32) * density).astype(jnp.bfloat16)

    def sums_block(i):
        place = block_rows(i)
        part[place, :] = jnp.dot(kbuf[place, :], points[...], preferred_element_type=jnp.float32)

    def first_turn(t, carry):
        stream(0, 0, t)
        stream(0, 1, t)
        gather_half(0, t)
        following = lax.div(t, per_block) + 1

        @pl.when((lax.rem(t, per_block) == 0) & (following < blocks))
        def _():
            kernel_block(following)

        @pl.when((lax.rem(t, per_block) == per_block - 1) & (following < blocks))
        def _():
            sums_block(following)

        return carry

    kernel_block(0)
    sums_block(0)
    lax.fori_loop(0, turn_two, first_turn, 0)

    def second_turn(t, carry):
        for h in range(2):
            u = t - begins[1][h]

            @pl.when((u >= 0) & (u < chunks) & (lax.rem(t, per_block) == 0))
            def _():
                place = block_rows(lax.div(u, per_block))
                part[place, h * half : (h + 1) * half] = jnp.dot(
                    kbuf[place, :], fields[h], preferred_element_type=jnp.float32
                )

        stream(1, 0, t)
        stream(1, 1, t)
        gather_half(1, t)
        return carry

    lax.fori_loop(turn_two, turn_two + chunks + span, second_turn, 0)

    def finish(c, carry):
        for turn in range(2):
            for h, owner in enumerate(owners):
                @pl.when(z < owner)
                def _():
                    reduce_copy(turn, h, 0, c, z + 1).wait_send()

                @pl.when(z > owner)
                def _():
                    reduce_copy(turn, h, 1, c, z - 1).wait_send()

                @pl.when((z <= owner) & (z > 0))
                def _():
                    result_copy(turn, h, 0, c, z - 1).wait_send()

                @pl.when((z >= owner) & (z < n - 1))
                def _():
                    result_copy(turn, h, 1, c, z + 1).wait_send()

        return carry

    lax.fori_loop(0, chunks, finish, 0)
    for g in range(3):
        gather_sent(g)


def filtered(n, slabs, fit, orbitals, table, pot, rows, places):
    cells, total = fit.shape
    columns = orbitals.shape[1]
    half = columns // 2
    count = rows.shape[0]
    chunks = cells // CHUNK
    vmem = pl.BlockSpec(memory_space=pltpu.VMEM)
    anywhere = pl.BlockSpec(memory_space=pl.ANY)
    bf16, f32, dma = jnp.bfloat16, jnp.float32, pltpu.SemaphoreType.DMA
    return pl.pallas_call(
        functools.partial(filter_kernel, n, slabs),
        out_shape=jax.ShapeDtypeStruct((2, cells, half), bf16),
        in_specs=[anywhere] * 3 + [vmem, vmem, pl.BlockSpec(memory_space=pltpu.SMEM)],
        out_specs=vmem,
        scratch_shapes=[
            pltpu.VMEM((cells, columns), bf16),
            pltpu.VMEM(table.shape, bf16),
            pltpu.VMEM((cells, total), bf16),
            pltpu.VMEM((count, cells), bf16),
            pltpu.VMEM((slabs, count + 2 * PAD, columns), bf16),
            pltpu.VMEM((slabs, count + 2 * PAD, half), bf16),
            pltpu.VMEM((slabs, count + 2 * PAD, half), bf16),
            pltpu.VMEM((total, columns), bf16),
            pltpu.VMEM((columns, total), bf16),
            pltpu.VMEM((2, total, half), bf16),
            pltpu.VMEM((2, cells, half), bf16),
            pltpu.VMEM((cells, columns), f32),
            pltpu.VMEM((2, cells + 2 * WIDTH * PLANE, half), bf16),
            pltpu.VMEM((cells, half), f32),
            pltpu.VMEM((2, 2, cells, half), bf16),
            pltpu.VMEM((2, 2, 2, cells, half), bf16),
            dma((2,)),
            dma((cells // BLOCK,)),
            dma((3, 2, slabs)),
            dma((3, 2, slabs)),
            dma((2, 2, chunks)),
            dma((2, 2, 2, chunks)),
            dma((2, 2, 2, chunks)),
            dma((2, 2, chunks)),
            dma((2, 2)),
            dma((2, 2)),
        ],
        compiler_params=pltpu.CompilerParams(
            collective_id=0, has_side_effects=True, vmem_limit_bytes=VMEM_LIMIT
        ),
        cost_estimate=pl.CostEstimate(
            flops=6 * cells * total * columns, bytes_accessed=2 * cells * total, transcendentals=0
        ),
    )(fit, orbitals, table, pot, rows, places)


def rows_kernel(counts, listed, rows, places, wide):
    z = lax.axis_index("pt")
    me = lax.axis_index("slab")
    slabs = counts.shape[1]
    capacity = listed.shape[2]
    count = rows.shape[0]
    width = places.shape[0] // slabs

    def one(s, carry):
        place, mine = carry
        start = lax.div(place, ALIGN)
        slot = lax.bitwise_xor(s, me) * width
        for b in range(width):
            begin = (b + 1) * (PAD // ALIGN) - start
            places[slot + b] = jnp.clip(begin, 0, (PAD + count) // ALIGN)
        mine = jnp.where(s == me, place, mine)
        return place + counts[z, s], mine

    _, mine = lax.fori_loop(0, slabs, one, (jnp.int32(0), jnp.int32(0)))
    lane = lax.broadcasted_iota(jnp.int32, (8, capacity), 1)
    value = jnp.broadcast_to(listed[z], (8, capacity))
    wide[...] = jnp.full(wide.shape, -1.0, jnp.float32)
    wide[:, :capacity] = jnp.where(lane < counts[z, me], value, -1).astype(jnp.float32)
    moved = pltpu.roll(wide[...], lax.rem(mine, ALIGN), 1)
    rows[...] = moved.T[:count, :1].astype(jnp.int32)


def shifted_rows(owner_rows, owner_count, total):
    slabs = owner_count.shape[1]
    count = owner_rows.shape[2] + ALIGN
    lanes = (count + 127) // 128 * 128
    smem = pl.BlockSpec(memory_space=pltpu.SMEM)
    vmem = pl.BlockSpec(memory_space=pltpu.VMEM)
    return pl.pallas_call(
        rows_kernel,
        out_shape=[
            jax.ShapeDtypeStruct((count, 1), jnp.int32),
            jax.ShapeDtypeStruct((slabs * (total // PAD),), jnp.int32),
        ],
        in_specs=[smem, vmem],
        out_specs=[vmem, smem],
        scratch_shapes=[pltpu.VMEM((8, lanes), jnp.float32)],
    )(owner_count, owner_rows)


def body(n, slabs, orbitals, potential, fit_matrix, owner_rows, owner_count):
    rows, places = shifted_rows(owner_rows, owner_count, fit_matrix.shape[1])
    pot = potential.reshape(-1, PLANE)
    table = jnp.asarray(plane_table())
    halves = filtered(n, slabs, fit_matrix, orbitals, table, pot, rows, places)
    return jnp.concatenate([halves[0], halves[1]], axis=1)


def solution(mesh):
    placed = (P("slab", None), P("slab"), P("slab", "pt"), P(None, "slab", None), P())
    return jax.shard_map(
        functools.partial(body, mesh.shape["pt"], mesh.shape["slab"]),
        mesh=mesh, in_specs=placed, out_specs=P("slab", None), check_vma=False,
    )
```
